256 devices in a mesh: loop: 4 (over y_lo, core), grp: 64 (over y_hi, z, x).
Axes of the slice: x: 4, y: 4 (y_hi: 2, y_lo: 2; y = y_hi * 2 + y_lo), z: 8, core: 2. Of those that a mesh axis runs over, the one named last changes fastest.
Arguments:
- queries: bfloat16 [1, 12, 16, 32, 128], P(None, None, 'loop'), may hold values from -18 to 18
- cache_keys: bfloat16 [1, 12, 131072, 128], P(None, None, ('loop', 'grp')), may hold values from -7 to 7
- cache_values: bfloat16 [1, 12, 131072, 128], P(None, None, ('loop', 'grp')), may hold values from -6 to 6
- draft_keys: bfloat16 [1, 12, 32, 128], replicated, may hold values from -18 to 18
- draft_values: bfloat16 [1, 12, 32, 128], replicated, may hold values from -6 to 6
- tree_mask: int32 [12, 32, 32], replicated, may hold values from 0 to 1, as said below
- valid_length: int32 [12], replicated, may hold values from 65536 to 131072
Outputs:
- attended: bfloat16 [1, 12, 16, 32, 128], P(None, None, 'loop')
The draws below stay inside these ranges and needn't reach their ends.
Inputs may be any that keep to these rules, and one draw needn't show every extreme that they name: `tree_mask`: row r of each sequence's mask holds 1 at column r and at the columns of every ancestor of draft token r in a tree whose parents precede their children, 0 elsewhere.
All inputs are finite; a program needn't handle non-finite values.
Results may differ from the reference program's by a relative error of at most 0.004.
Values may be sent and summed in bfloat16 or wider, within the bound.
A program may use at most 256 MiB of HBM per device.

```python
import math
import jax
import jax.numpy as jnp
from jax import lax

H = 16
DH = 128
R = 32
LAYERS = 1
SEQS = 12
CTX_SEQ = 131072


def draw_cache_keys(key, part):
    key = jax.random.fold_in(key, 3)
    entries = jnp.clip(jax.random.normal(key, (LAYERS, SEQS, CTX_SEQ, DH), jnp.float32), -7.0, 7.0)
    return entries.astype(jnp.bfloat16)


def draw_queries(key, part):
    key = jax.random.fold_in(key, 5)
    entries = jnp.clip(3.5 * jax.random.normal(key, (LAYERS, SEQS, H, R, DH), jnp.float32), -14.0, 14.0)
    return entries.astype(jnp.bfloat16)


def draw_tree_mask(key, part):
    key = jax.random.fold_in(key, 11)
    picks = jax.random.randint(key, (SEQS, R), 0, 1 << 20)
    places = jnp.arange(R, dtype=jnp.int32)
    parents = jnp.where(places[None, :] > 0, picks % jnp.maximum(places, 1)[None, :], 0).astype(jnp.int32)
    start = jnp.broadcast_to((places[:, None] == places[None, :]).astype(jnp.int32), (SEQS, R, R))
    chain_start = jnp.broadcast_to(places[None, :], (SEQS, R)).astype(jnp.int32)

    def climb(index, carry):
        chain, marks = carry
        chain = jnp.take_along_axis(parents, chain, axis=1).astype(jnp.int32)
        marks = jnp.maximum(marks, (chain[:, :, None] == places[None, None, :]).astype(jnp.int32))
        return (chain, marks)
    chain, marks = lax.fori_loop(0, R, climb, (chain_start, start))
    return marks


def place_ends(drawn, rng, smallest, top_value):
    shape = drawn.shape
    place = [jax.random.randint(jax.random.fold_in(rng, axis), (), 0, shape[axis]) for axis in range(len(shape))]
    drawn = drawn.at[tuple(place)].set(smallest)
    longest = shape.index(max(shape))
    place[longest] = (place[longest] + 1) % shape[longest]
    return drawn.at[tuple(place)].set(top_value)


def block_levels(own_key, dims, cuts, smallest, largest):
    factor_of = 1.0
    for axis_at, parts in cuts:
        steps = jax.random.uniform(jax.random.fold_in(jax.random.fold_in(own_key, 6), axis_at), (parts,), jnp.float32, smallest / len(cuts), largest / len(cuts))
        factor_of = factor_of * jnp.repeat(jnp.exp(steps), dims[axis_at] // parts).reshape((-1,) + (1,) * (len(dims) - 1 - axis_at))
    return factor_of


def noise(rng, extent, width, most, shards=(), held_as=jnp.bfloat16):
    values = width * jax.random.normal(rng, extent, jnp.float32)
    if shards:
        values = values * block_levels(rng, extent, shards, -0.22, 0.18)
    return jnp.clip(values, -most, most).astype(held_as)


def setup_inputs(seed: int = 0) -> dict:
    streams_of = jax.random.split(jax.random.key(seed), 8)
    queries = draw_queries(jax.random.fold_in(streams_of[7], 71), 0)
    cache_keys = draw_cache_keys(jax.random.fold_in(streams_of[7], 71), 0)
    cache_values = noise(streams_of[2], (LAYERS, SEQS, CTX_SEQ, DH), 1.0, 6.0, ((2, 256),))
    draft_keys = noise(streams_of[3], (LAYERS, SEQS, R, DH), 3.0, 18.0)
    draft_values = noise(streams_of[4], (LAYERS, SEQS, R, DH), 1.0, 6.0)
    tree_mask = draw_tree_mask(jax.random.fold_in(streams_of[7], 71), 0)
    valid_length = place_ends(jax.random.randint(streams_of[6], (SEQS,), CTX_SEQ // 2, CTX_SEQ + 1), jax.random.fold_in(streams_of[6], 1), CTX_SEQ // 2, CTX_SEQ).astype(jnp.int32)
    return dict(queries=queries, cache_keys=cache_keys, cache_values=cache_values, draft_keys=draft_keys, draft_values=draft_values, tree_mask=tree_mask, valid_length=valid_length)


FLOOR = -1e+30

def one_sequence(items):
    query_block, key_rows, value_rows, draft_key_rows, draft_value_rows, mask_rows, limit = items
    scale = 1.0 / math.sqrt(DH)
    block = math.gcd(CTX_SEQ, 8192)
    count = CTX_SEQ // block
    allowed = jnp.tile(mask_rows, (H, 1)) == 1
    query_rows = query_block.reshape(H * R, DH)
    tree_scores = jnp.dot(query_rows, draft_key_rows.T, preferred_element_type=jnp.float32) * scale
    peak = lax.optimization_barrier(jnp.max(jnp.where(allowed, tree_scores, FLOOR), axis=1))
    weights = jnp.where(allowed, jnp.exp(tree_scores - peak[:, None]), 0.0).astype(jnp.bfloat16)
    total = lax.optimization_barrier(jnp.sum(weights.astype(jnp.float32), axis=1))
    summed = jnp.dot(weights, draft_value_rows, preferred_element_type=jnp.float32)
    key_blocks = key_rows.reshape(count, block, DH)
    value_blocks = value_rows.reshape(count, block, DH)

    def visit(carry, item):
        run_peak, run_total, run_sum = carry
        key_block, value_block, block_index = item
        positions = block_index * block + lax.iota(jnp.int32, block)
        usable = (positions < limit)[None, :]
        scores = jnp.dot(query_rows, key_block.T, preferred_element_type=jnp.float32) * scale
        block_peak = lax.optimization_barrier(jnp.max(jnp.where(usable, scores, FLOOR), axis=1))
        joined = jnp.maximum(run_peak, block_peak)
        factor = jnp.exp(run_peak - joined)
        block_weights = jnp.where(usable, jnp.exp(scores - joined[:, None]), 0.0).astype(jnp.bfloat16)
        new_total = run_total * factor + lax.optimization_barrier(jnp.sum(block_weights.astype(jnp.float32), axis=1))
        new_sum = run_sum * factor[:, None] + jnp.dot(block_weights, value_block, preferred_element_type=jnp.float32)
        return ((joined, new_total, new_sum), None)
    (peak, total, summed), unused = lax.scan(visit, (peak, total, summed), (key_blocks, value_blocks, jnp.arange(count, dtype=jnp.int32)))
    return (summed / total[:, None]).astype(jnp.bfloat16).reshape(H, R, DH)

def reference(queries, cache_keys, cache_values, draft_keys, draft_values, tree_mask, valid_length):
    results = []
    for layer_index in range(LAYERS):
        results.append(lax.map(one_sequence, (queries[layer_index], cache_keys[layer_index], cache_values[layer_index], draft_keys[layer_index], draft_values[layer_index], tree_mask, valid_length)))
    return jnp.stack(results, axis=0)
```

```python
import functools
import math

import jax
import jax.numpy as jnp
from jax import lax
from jax.experimental import pallas as pl
from jax.experimental.pallas import tpu as pltpu
from jax.sharding import PartitionSpec as P

MESH = pl.DeviceIdType.MESH
F32 = jnp.float32
BF16 = jnp.bfloat16

SEQS = 12
ROWS = 128
KEYS = 512
WIDTH = 128
DRAFT = 32
NX, NY, NZ = 4, 4, 8
CHUNKS = 3
PER = SEQS // CHUNKS
PIECE = 16
SPAN = PER * PIECE
SLICE = SPAN // NZ
NEAR = [(dx, dy) for dy in (0, 2) for dx in range(NX) if (dx, dy) != (0, 0)]
FAR = [(dx, dy) for dy in (1, 3) for dx in range(NX)]
PLANE = NEAR + FAR

SCALE = math.log2(math.e) / math.sqrt(WIDTH)
FLOOR = -1e30
LOW = -1e29


def iota(shape, axis):
    return lax.broadcasted_iota(jnp.int32, shape, axis)


def to_row(column):
    eye = iota((ROWS, ROWS), 0) == iota((ROWS, ROWS), 1)
    return jnp.sum(jnp.where(eye, column, 0.0), axis=0, keepdims=True)


def to_column(row, rows, first):
    pick = iota((rows, ROWS), 1) == iota((rows, ROWS), 0) + first
    return jnp.sum(jnp.where(pick, row, 0.0), axis=1, keepdims=True)


def by_piece(tile):
    lane = iota((8, ROWS), 1) // PIECE
    sub = iota((8, ROWS), 0)
    out = jnp.zeros((8, ROWS), F32)
    for d in range(8):
        moved = tile if d == 0 else pltpu.roll(tile, PIECE * d, 1)
        diagonal = jnp.sum(jnp.where(lane == sub, moved, 0.0), axis=0, keepdims=True)
        out = jnp.where((lane - sub + 8) % 8 == d, diagonal, out)
    return out


def kernel(
    q_hbm, k_hbm, v_hbm, dk_hbm, dv_hbm, tm_hbm, vl_hbm, out_ref,
    Q, K, V, DK, DV, TM, VL,
    own, own_s, give, give_s, got, got_s,
    plane, plane_s, land, land_s,
    zed, zed_s, zland, zland_s, done,
    ld, ld_small, q_send, q_recv, c_send, c_recv, a_send, a_recv, z_send, z_recv, g_send, g_recv, o_send, o_recv,
):
    loop_index = lax.axis_index("loop")
    group_index = lax.axis_index("grp")
    core = loop_index % 2
    x = group_index % NX
    z = (group_index // NX) % NZ
    y = (group_index // (NX * NZ)) * 2 + loop_index // 2

    def device(px, py, pz, pc):
        return ((py % 2) * 2 + pc, ((py // 2) * NZ + pz) * NX + px)

    mate = device(x, y, z, 1 - core)

    def in_plane(dx, dy):
        return device((x + dx) % NX, (y + dy) % NY, z, core)

    def along_z(dz):
        return device(x, y, (z + dz) % NZ, core)

    def piece_of(px, py):
        return (py // 2) * NX + px

    mine = piece_of(x, y)

    def remote(src, dst, send, recv, target):
        return pltpu.make_async_remote_copy(
            src_ref=src, dst_ref=dst, send_sem=send, recv_sem=recv, device_id=target, device_id_type=MESH
        )

    peers = [mate] + [in_plane(dx, dy) for dx, dy in PLANE] + [along_z(dz) for dz in range(1, NZ)]
    barrier = pltpu.get_barrier_semaphore()
    for peer in peers:
        pl.semaphore_signal(barrier, inc=1, device_id=peer, device_id_type=MESH)

    def seqs(c):
        return pl.ds(c * PER, PER)

    def load(c):
        return [
            pltpu.make_async_copy(q_hbm.at[seqs(c)], Q.at[0, seqs(c)], ld.at[c, 0]),
            pltpu.make_async_copy(k_hbm.at[seqs(c)], K.at[seqs(c)], ld.at[c, 1]),
            pltpu.make_async_copy(v_hbm.at[seqs(c)], V.at[seqs(c)], ld.at[c, 2]),
        ]

    small = [
        pltpu.make_async_copy(vl_hbm, VL, ld_small.at[0]),
        pltpu.make_async_copy(dk_hbm, DK, ld_small.at[1]),
        pltpu.make_async_copy(dv_hbm, DV, ld_small.at[2]),
        pltpu.make_async_copy(tm_hbm, TM, ld_small.at[3]),
    ]
    small[0].start()
    for c in range(CHUNKS):
        for copy in load(c):
            copy.start()
    for copy in small[1:]:
        copy.start()

    half = ROWS // 2

    def ask_mate(c):
        return remote(q_hbm.at[seqs(c)], Q.at[1, seqs(c)], q_send.at[c, 0], q_recv.at[c, 0], mate)

    def ask_far(c, side):
        rows = pl.ds(side * half, half)
        return remote(
            q_hbm.at[seqs(c), rows], Q.at[2, seqs(c), rows], q_send.at[c, 1 + side], q_recv.at[c, 1 + side],
            in_plane(0, 1 if side == 0 else 3),
        )

    def pass_on(c):
        return remote(Q.at[2, seqs(c)], Q.at[3, seqs(c)], q_send.at[c, 3], q_recv.at[c, 3], mate)

    first = (loop_index * (NX * 2 * NZ) + group_index) * KEYS
    position = first + iota((1, KEYS), 1)
    ones = jnp.ones((KEYS, WIDTH), BF16)
    sub8 = iota((8, ROWS), 0)

    def attend(j, c, sums, figures, side):
        def one(i, tile):
            s = c * PER + i
            scores = lax.dot_general(Q[j, s], K[s], (((1,), (1,)), ((), ())), preferred_element_type=F32)
            scores = jnp.where(position < VL[s], scores * SCALE, FLOOR)
            peak = jnp.maximum(jnp.max(scores, axis=1, keepdims=True), LOW)
            weights = jnp.exp2(scores - peak).astype(BF16)
            both = jnp.dot(weights, jnp.concatenate([V[s], ones], axis=1), preferred_element_type=F32)
            sums[side, s] = both[:, :WIDTH].astype(sums.dtype)
            tile = jnp.where(sub8 == i, to_row(peak), tile)
            return jnp.where(sub8 == PER + i, to_row(both[:, WIDTH:]), tile)

        figures[side, c] = lax.fori_loop(0, PER, one, jnp.zeros((8, ROWS), F32))

    def swap(side, c):
        return [
            remote(give.at[side, seqs(c)], got.at[side, seqs(c)], c_send.at[side, c, 0], c_recv.at[side, c, 0], mate),
            remote(give_s.at[side, c], got_s.at[side, c], c_send.at[side, c, 1], c_recv.at[side, c, 1], mate),
        ]

    def merge_cores(side, c):
        for copy in swap(side, c):
            copy.wait_recv()
        a, b = own_s[side, c], got_s[side, c]
        is_peak = sub8 < PER
        joined = jnp.maximum(a, b)
        fa = jnp.exp2(jnp.where(is_peak, a - joined, 0.0))
        fb = jnp.exp2(jnp.where(is_peak, b - joined, 0.0))
        total = pltpu.roll(fa, PER, 0) * a + pltpu.roll(fb, PER, 0) * b
        pieces = by_piece(jnp.where(is_peak, joined, total))
        for p in range(8):
            plane_s[side, c, p] = pieces[p : p + 1]

        for i in range(PER):
            s = c * PER + i
            plane[side, s] = (
                own[side, s] * to_column(fa[i : i + 1], ROWS, 0)
                + got[side, s].astype(F32) * to_column(fb[i : i + 1], ROWS, 0)
            ).astype(BF16)

    def scatter(side, c):
        copies = []
        for n, (dx, dy) in enumerate(PLANE):
            if (dy % 2) != side:
                continue
            piece = piece_of((x + dx) % NX, (y + dy) % NY)
            rows = pl.ds(pl.multiple_of(piece * PIECE, PIECE), PIECE)
            target = in_plane(dx, dy)
            copies.append(remote(plane.at[side, seqs(c), rows], land.at[c, n], a_send.at[c, n, 0], a_recv.at[c, n, 0], target))
            copies.append(remote(plane_s.at[side, c, piece], land_s.at[c, n], a_send.at[c, n, 1], a_recv.at[c, n, 1], target))
        return copies

    def merge_plane(c):
        for side in range(2):
            for copy in scatter(side, c):
                copy.wait_recv()
        figures = jnp.concatenate([plane_s[0, c, mine]] + [land_s[c, n] for n in range(len(PLANE))], axis=0)
        peak = jnp.max(figures, axis=0, keepdims=True)
        is_peak = iota((1, ROWS), 1) < SPAN
        factor = jnp.exp2(jnp.where(is_peak, figures - peak, 0.0))
        total = jnp.sum(pltpu.roll(factor, SPAN, 1) * figures, axis=0, keepdims=True)
        zed_s[c] = jnp.where(is_peak, peak, total)
        rows = pl.ds(pl.multiple_of(mine * PIECE, PIECE), PIECE)
        acc = plane[0, seqs(c), rows].reshape(SPAN, WIDTH).astype(F32) * to_column(factor[0:1], SPAN, 0)
        for n in range(len(PLANE)):
            acc += land[c, n].reshape(SPAN, WIDTH).astype(F32) * to_column(factor[n + 1 : n + 2], SPAN, 0)
        zed[c] = acc.reshape(NZ, SLICE, WIDTH)

    def spread(c):
        copies = []
        for dz in range(1, NZ):
            target = along_z(dz)
            copies.append(remote(zed.at[c, (z + dz) % NZ], zland.at[c, dz - 1], z_send.at[c, dz, 0], z_recv.at[c, dz, 0], target))
            copies.append(remote(zed_s.at[c], zland_s.at[c, dz - 1], z_send.at[c, dz, 1], z_recv.at[c, dz, 1], target))
        return copies

    def draft(c):
        s = c * PER + z // 2
        rows = pl.ds(pl.multiple_of(mine * PIECE, PIECE), PIECE)
        scores = lax.dot_general(Q[0, s, rows], DK[s], (((1,), (1,)), ((), ())), preferred_element_type=F32) * SCALE
        allowed = TM[s, pl.ds(pl.multiple_of((mine % 2) * PIECE, PIECE), PIECE)] == 1
        peak = jnp.max(jnp.where(allowed, scores, FLOOR), axis=1, keepdims=True)
        weights = jnp.where(allowed, jnp.exp2(scores - peak), 0.0).astype(BF16)
        total = jnp.sum(weights.astype(F32), axis=1, keepdims=True)
        sums = jnp.dot(weights, DV[s], preferred_element_type=F32)
        low = z % 2 == 0
        return tuple(jnp.where(low, a[:SLICE], a[SLICE:]) for a in (peak, total, sums))

    def finish(c, drafted):
        for copy in spread(c):
            copy.wait_recv()
        figures = jnp.concatenate([zed_s[c]] + [zland_s[c, n] for n in range(NZ - 1)], axis=0)
        peak = jnp.max(figures, axis=0, keepdims=True)
        is_peak = iota((1, ROWS), 1) < SPAN
        factor = jnp.exp2(jnp.where(is_peak, figures - peak, 0.0))
        total = jnp.sum(pltpu.roll(factor, SPAN, 1) * figures, axis=0, keepdims=True)
        here = z * SLICE
        acc = zed[c, z] * to_column(factor[0:1], SLICE, here)
        for n in range(NZ - 1):
            acc += zland[c, n] * to_column(factor[n + 1 : n + 2], SLICE, here)
        top = to_column(peak, SLICE, here)
        tot = to_column(total, SLICE, here + SPAN)
        d_top, d_tot, d_acc = drafted
        joined = jnp.maximum(top, d_top)
        fa, fb = jnp.exp2(top - joined), jnp.exp2(d_top - joined)
        done[c, z] = (acc * fa + d_acc * fb) / (tot * fa + d_tot * fb)

    def regather(c):
        return [
            remote(done.at[c, z], done.at[c, z], g_send.at[c, dz], g_recv.at[c, dz], along_z(dz)) for dz in range(1, NZ)
        ]

    def regathered(c):
        for dz in range(1, NZ):
            source = (z + NZ - dz) % NZ
            remote(done.at[c, z], done.at[c, source], g_send.at[c, dz], g_recv.at[c, dz], along_z(dz)).wait_recv()

    def deliver(c):
        rows = pl.ds(pl.multiple_of(mine * PIECE, PIECE), PIECE)
        part = out_ref.at[seqs(c), rows]
        return [
            remote(part, part, o_send.at[c, n], o_recv.at[c, n], in_plane(dx, dy)) for n, (dx, dy) in enumerate(NEAR)
        ]

    def delivered(c):
        rows = pl.ds(pl.multiple_of(mine * PIECE, PIECE), PIECE)
        for n, (dx, dy) in enumerate(NEAR):
            source = piece_of((x + NX - dx) % NX, (y + NY - dy) % NY)
            there = pl.ds(pl.multiple_of(source * PIECE, PIECE), PIECE)
            remote(
                out_ref.at[seqs(c), rows], out_ref.at[seqs(c), there], o_send.at[c, n], o_recv.at[c, n], in_plane(dx, dy)
            ).wait_recv()

    def start(copies):
        for copy in copies:
            copy.start()

    pl.semaphore_wait(barrier, len(peers))
    for c in range(CHUNKS):
        for side in range(2):
            ask_far(c, side).start()
    for c in range(CHUNKS):
        ask_mate(c).start()

    small[0].wait()

    def near_own(c, carry):
        for copy in load(c):
            copy.wait()
        attend(0, c, own, own_s, 0)
        return carry

    def near_mate(c, carry):
        ask_mate(c).wait_recv()
        attend(1, c, give, give_s, 0)
        start(swap(0, c))
        return carry

    def near_merge(c, carry):
        merge_cores(0, c)
        start(scatter(0, c))
        return carry

    def far_own(c):
        for side in range(2):
            ask_far(c, side).wait_recv()
        pass_on(c).start()
        attend(2, c, own, own_s, 1)

    def far_mate(c):
        pass_on(c).wait_recv()
        attend(3, c, give, give_s, 1)
        start(swap(1, c))

    def far_merge(c):
        merge_cores(1, c)
        start(scatter(1, c))

    lax.fori_loop(0, CHUNKS, near_own, 0)
    lax.fori_loop(0, CHUNKS, near_mate, 0)
    lax.fori_loop(0, CHUNKS, near_merge, 0)

    def far(c, carry):
        far_own(c)
        far_mate(c)
        return carry

    def far2(c, carry):
        far_merge(c)
        return carry

    lax.fori_loop(0, CHUNKS, far, 0)
    lax.fori_loop(0, CHUNKS, far2, 0)

    for copy in small[1:]:
        copy.wait()
    drafted = [draft(c) for c in range(CHUNKS)]

    for c in range(CHUNKS):
        merge_plane(c)
        start(spread(c))
    for c in range(CHUNKS):
        finish(c, drafted[c])
        start(regather(c))
    for c in range(CHUNKS):
        regathered(c)
        rows = pl.ds(pl.multiple_of(mine * PIECE, PIECE), PIECE)
        out_ref[seqs(c), rows] = done[c].reshape(PER, PIECE, WIDTH).astype(BF16)
        start(deliver(c))

    for c in range(CHUNKS):
        sent = [ask_mate(c), ask_far(c, 0), ask_far(c, 1), pass_on(c)]
        sent += swap(0, c) + swap(1, c) + scatter(0, c) + scatter(1, c) + spread(c) + regather(c) + deliver(c)
        for copy in sent:
            copy.wait_send()
        delivered(c)


def local(queries, cache_keys, cache_values, draft_keys, draft_values, tree_mask, valid_length):
    dma = pltpu.SemaphoreType.DMA
    n = len(PLANE)
    scratch = [
        pltpu.VMEM((4, SEQS, ROWS, WIDTH), BF16),
        pltpu.VMEM((SEQS, KEYS, WIDTH), BF16),
        pltpu.VMEM((SEQS, KEYS, WIDTH), BF16),
        pltpu.VMEM((SEQS, DRAFT, WIDTH), BF16),
        pltpu.VMEM((SEQS, DRAFT, WIDTH), BF16),
        pltpu.VMEM((SEQS, DRAFT, DRAFT), jnp.int32),
        pltpu.SMEM((SEQS,), jnp.int32),
        pltpu.VMEM((2, SEQS, ROWS, WIDTH), F32),
        pltpu.VMEM((2, CHUNKS, 8, ROWS), F32),
        pltpu.VMEM((2, SEQS, ROWS, WIDTH), BF16),
        pltpu.VMEM((2, CHUNKS, 8, ROWS), F32),
        pltpu.VMEM((2, SEQS, ROWS, WIDTH), BF16),
        pltpu.VMEM((2, CHUNKS, 8, ROWS), F32),
        pltpu.VMEM((2, SEQS, ROWS, WIDTH), BF16),
        pltpu.VMEM((2, CHUNKS, 8, 1, ROWS), F32),
        pltpu.VMEM((CHUNKS, n, PER, PIECE, WIDTH), BF16),
        pltpu.VMEM((CHUNKS, n, 1, ROWS), F32),
        pltpu.VMEM((CHUNKS, NZ, SLICE, WIDTH), F32),
        pltpu.VMEM((CHUNKS, 1, ROWS), F32),
        pltpu.VMEM((CHUNKS, NZ - 1, SLICE, WIDTH), F32),
        pltpu.VMEM((CHUNKS, NZ - 1, 1, ROWS), F32),
        pltpu.VMEM((CHUNKS, NZ, SLICE, WIDTH), F32),
        dma((CHUNKS, 3)),
        dma((4,)),
        dma((CHUNKS, 4)),
        dma((CHUNKS, 4)),
        dma((2, CHUNKS, 2)),
        dma((2, CHUNKS, 2)),
        dma((CHUNKS, n, 2)),
        dma((CHUNKS, n, 2)),
        dma((CHUNKS, NZ, 2)),
        dma((CHUNKS, NZ, 2)),
        dma((CHUNKS, NZ)),
        dma((CHUNKS, NZ)),
        dma((CHUNKS, len(NEAR))),
        dma((CHUNKS, len(NEAR))),
    ]
    out = pl.pallas_call(
        kernel,
        out_shape=jax.ShapeDtypeStruct((SEQS, ROWS, WIDTH), BF16),
        in_specs=[pl.BlockSpec(memory_space=pltpu.HBM)] * 7,
        out_specs=pl.BlockSpec(memory_space=pltpu.VMEM),
        scratch_shapes=scratch,
        compiler_params=pltpu.CompilerParams(collective_id=0, has_side_effects=True, vmem_limit_bytes=48 << 20),
        name="attend",
    )(
        queries.reshape(SEQS, ROWS, WIDTH),
        cache_keys.reshape(SEQS, KEYS, WIDTH),
        cache_values.reshape(SEQS, KEYS, WIDTH),
        draft_keys.reshape(SEQS, DRAFT, WIDTH),
        draft_values.reshape(SEQS, DRAFT, WIDTH),
        tree_mask,
        valid_length,
    )
    return out.reshape(queries.shape)


def solution(mesh):
    in_specs = (
        P(None, None, "loop", None, None),
        P(None, None, ("loop", "grp"), None),
        P(None, None, ("loop", "grp"), None),
        P(),
        P(),
        P(),
        P(),
    )
    out_specs = P(None, None, "loop", None, None)
    return jax.shard_map(local, mesh=mesh, in_specs=in_specs, out_specs=out_specs, check_vma=False)
```

```python
import functools
import math

import jax
import jax.numpy as jnp
from jax import lax
from jax.experimental import pallas as pl
from jax.experimental.pallas import tpu as pltpu
from jax.sharding import PartitionSpec as P

MESH = pl.DeviceIdType.MESH
F32 = jnp.float32
BF16 = jnp.bfloat16

SEQS = 12
ROWS = 128
KEYS = 512
WIDTH = 128
DRAFT = 32
NX, NY, NZ = 4, 4, 8
CHUNKS = 3
PER = SEQS // CHUNKS
PIECE = 16
SPAN = PER * PIECE
SLICE = SPAN // NZ
NEAR = [(dx, dy) for dy in (0, 2) for dx in range(NX) if (dx, dy) != (0, 0)]
FAR = [(dx, dy) for dy in (1, 3) for dx in range(NX)]
PLANE = NEAR + FAR

SCALE = math.log2(math.e) / math.sqrt(WIDTH)
FLOOR = -1e30
LOW = -1e29


def iota(shape, axis):
    return lax.broadcasted_iota(jnp.int32, shape, axis)


def to_row(column):
    eye = iota((ROWS, ROWS), 0) == iota((ROWS, ROWS), 1)
    return jnp.sum(jnp.where(eye, column, 0.0), axis=0, keepdims=True)


def to_column(row, rows, first):
    pick = iota((rows, ROWS), 1) == iota((rows, ROWS), 0) + first
    return jnp.sum(jnp.where(pick, row, 0.0), axis=1, keepdims=True)


def by_piece(tile):
    lane = iota((8, ROWS), 1) // PIECE
    sub = iota((8, ROWS), 0)
    out = jnp.zeros((8, ROWS), F32)
    for d in range(8):
        moved = tile if d == 0 else pltpu.roll(tile, PIECE * d, 1)
        diagonal = jnp.sum(jnp.where(lane == sub, moved, 0.0), axis=0, keepdims=True)
        out = jnp.where((lane - sub + 8) % 8 == d, diagonal, out)
    return out


def kernel(
    q_hbm, k_hbm, v_hbm, dk_hbm, dv_hbm, tm_hbm, vl_hbm, out_ref,
    Q, K, V, DK, DV, TM, VL,
    own, own_s, give, give_s, got, got_s,
    plane, plane_s, land, land_s,
    zed, zed_s, zland, zland_s, done,
    ld, ld_small, q_send, q_recv, c_send, c_recv, a_send, a_recv, z_send, z_recv, g_send, g_recv, o_send, o_recv,
):
    loop_index = lax.axis_index("loop")
    group_index = lax.axis_index("grp")
    core = loop_index % 2
    x = group_index % NX
    z = (group_index // NX) % NZ
    y = (group_index // (NX * NZ)) * 2 + loop_index // 2

    def device(px, py, pz, pc):
        return ((py % 2) * 2 + pc, ((py // 2) * NZ + pz) * NX + px)

    mate = device(x, y, z, 1 - core)

    def in_plane(dx, dy):
        return device((x + dx) % NX, (y + dy) % NY, z, core)

    def along_z(dz):
        return device(x, y, (z + dz) % NZ, core)

    def piece_of(px, py):
        return (py // 2) * NX + px

    mine = piece_of(x, y)

    def remote(src, dst, send, recv, target):
        return pltpu.make_async_remote_copy(
            src_ref=src, dst_ref=dst, send_sem=send, recv_sem=recv, device_id=target, device_id_type=MESH
        )

    peers = [mate] + [in_plane(dx, dy) for dx, dy in PLANE] + [along_z(dz) for dz in range(1, NZ)]
    barrier = pltpu.get_barrier_semaphore()
    for peer in peers:
        pl.semaphore_signal(barrier, inc=1, device_id=peer, device_id_type=MESH)

    def seqs(c):
        return pl.ds(c * PER, PER)

    def load(c):
        return [
            pltpu.make_async_copy(q_hbm.at[seqs(c)], Q.at[0, seqs(c)], ld.at[c, 0]),
            pltpu.make_async_copy(k_hbm.at[seqs(c)], K.at[seqs(c)], ld.at[c, 1]),
            pltpu.make_async_copy(v_hbm.at[seqs(c)], V.at[seqs(c)], ld.at[c, 2]),
        ]

    small = [
        pltpu.make_async_copy(vl_hbm, VL, ld_small.at[0]),
        pltpu.make_async_copy(dk_hbm, DK, ld_small.at[1]),
        pltpu.make_async_copy(dv_hbm, DV, ld_small.at[2]),
        pltpu.make_async_copy(tm_hbm, TM, ld_small.at[3]),
    ]
    small[0].start()
    for c in range(CHUNKS):
        for copy in load(c):
            copy.start()
    for copy in small[1:]:
        copy.start()

    half = ROWS // 2

    def ask_mate(c):
        return remote(q_hbm.at[seqs(c)], Q.at[1, seqs(c)], q_send.at[0], q_recv.at[0, c], mate)

    def ask_far(c, side):
        rows = pl.ds(side * half, half)
        return remote(
            q_hbm.at[seqs(c), rows], Q.at[2, seqs(c), rows], q_send.at[1], q_recv.at[1, c],
            in_plane(0, 1 if side == 0 else 3),
        )

    def pass_on(c):
        return remote(Q.at[2, seqs(c)], Q.at[3, seqs(c)], q_send.at[2], q_recv.at[2, c], mate)

    def await_far(c):
        remote(Q.at[2, seqs(c)], Q.at[2, seqs(c)], q_send.at[1], q_recv.at[1, c], mate).wait_recv()

    first = (loop_index * (NX * 2 * NZ) + group_index) * KEYS
    position = first + iota((1, KEYS), 1)
    ones = jnp.ones((KEYS, WIDTH), BF16)
    sub8 = iota((8, ROWS), 0)

    def attend(j, c, sums, figures, side):
        def one(i, tile):
            s = c * PER + i
            scores = lax.dot_general(Q[j, s], K[s], (((1,), (1,)), ((), ())), preferred_element_type=F32)
            scores = jnp.where(position < VL[s], scores * SCALE, FLOOR)
            peak = jnp.maximum(jnp.max(scores, axis=1, keepdims=True), LOW)
            weights = jnp.exp2(scores - peak).astype(BF16)
            both = jnp.dot(weights, jnp.concatenate([V[s], ones], axis=1), preferred_element_type=F32)
            sums[side, s] = both[:, :WIDTH].astype(sums.dtype)
            tile = jnp.where(sub8 == i, to_row(peak), tile)
            return jnp.where(sub8 == PER + i, to_row(both[:, WIDTH:]), tile)

        figures[side, c] = lax.fori_loop(0, PER, one, jnp.zeros((8, ROWS), F32), unroll=PER)

    def swap(side, c):
        return [
            remote(give.at[side, seqs(c)], got.at[side, seqs(c)], c_send.at[0], c_recv.at[side, c, 0], mate),
            remote(give_s.at[side, c], got_s.at[side, c], c_send.at[1], c_recv.at[side, c, 1], mate),
        ]

    def merge_cores(side, c):
        for copy in swap(side, c):
            copy.wait_recv()
        a, b = own_s[side, c], got_s[side, c]
        is_peak = sub8 < PER
        joined = jnp.maximum(a, b)
        fa = jnp.exp2(jnp.where(is_peak, a - joined, 0.0))
        fb = jnp.exp2(jnp.where(is_peak, b - joined, 0.0))
        total = pltpu.roll(fa, PER, 0) * a + pltpu.roll(fb, PER, 0) * b
        pieces = by_piece(jnp.where(is_peak, joined, total))
        for p in range(8):
            plane_s[side, c, p] = pieces[p : p + 1]

        for i in range(PER):
            s = c * PER + i
            plane[side, s] = (
                own[side, s] * to_column(fa[i : i + 1], ROWS, 0)
                + got[side, s].astype(F32) * to_column(fb[i : i + 1], ROWS, 0)
            ).astype(BF16)

    def scatter(side, c):
        copies = []
        for n, (dx, dy) in enumerate(PLANE):
            if (dy % 2) != side:
                continue
            piece = piece_of((x + dx) % NX, (y + dy) % NY)
            rows = pl.ds(pl.multiple_of(piece * PIECE, PIECE), PIECE)
            target = in_plane(dx, dy)
            copies.append(remote(plane.at[side, seqs(c), rows], land.at[c, n], a_send.at[0], a_recv.at[c, 0], target))
            copies.append(remote(plane_s.at[side, c, piece], land_s.at[c, n], a_send.at[1], a_recv.at[c, 1], target))
        return copies

    def merge_plane(c):
        remote(land.at[c], land.at[c], a_send.at[0], a_recv.at[c, 0], mate).wait_recv()
        remote(land_s.at[c], land_s.at[c], a_send.at[1], a_recv.at[c, 1], mate).wait_recv()
        figures = jnp.concatenate([plane_s[0, c, mine]] + [land_s[c, n] for n in range(len(PLANE))], axis=0)
        peak = jnp.max(figures, axis=0, keepdims=True)
        is_peak = iota((1, ROWS), 1) < SPAN
        factor = jnp.exp2(jnp.where(is_peak, figures - peak, 0.0))
        total = jnp.sum(pltpu.roll(factor, SPAN, 1) * figures, axis=0, keepdims=True)
        zed_s[c] = jnp.where(is_peak, peak, total)
        rows = pl.ds(pl.multiple_of(mine * PIECE, PIECE), PIECE)
        acc = plane[0, seqs(c), rows].reshape(SPAN, WIDTH).astype(F32) * to_column(factor[0:1], SPAN, 0)
        for n in range(len(PLANE)):
            acc += land[c, n].reshape(SPAN, WIDTH).astype(F32) * to_column(factor[n + 1 : n + 2], SPAN, 0)
        zed[c] = acc.reshape(NZ, SLICE, WIDTH)

    def spread(c):
        copies = []
        for dz in range(1, NZ):
            target = along_z(dz)
            copies.append(remote(zed.at[c, (z + dz) % NZ], zland.at[c, dz - 1], z_send.at[0], z_recv.at[c, 0], target))
            copies.append(remote(zed_s.at[c], zland_s.at[c, dz - 1], z_send.at[1], z_recv.at[c, 1], target))
        return copies

    def draft(c):
        s = c * PER + z // 2
        rows = pl.ds(pl.multiple_of(mine * PIECE, PIECE), PIECE)
        scores = lax.dot_general(Q[0, s, rows], DK[s], (((1,), (1,)), ((), ())), preferred_element_type=F32) * SCALE
        allowed = TM[s, pl.ds(pl.multiple_of((mine % 2) * PIECE, PIECE), PIECE)] == 1
        peak = jnp.max(jnp.where(allowed, scores, FLOOR), axis=1, keepdims=True)
        weights = jnp.where(allowed, jnp.exp2(scores - peak), 0.0).astype(BF16)
        total = jnp.sum(weights.astype(F32), axis=1, keepdims=True)
        sums = jnp.dot(weights, DV[s], preferred_element_type=F32)
        low = z % 2 == 0
        return tuple(jnp.where(low, a[:SLICE], a[SLICE:]) for a in (peak, total, sums))

    def finish(c, drafted):
        remote(zland.at[c], zland.at[c], z_send.at[0], z_recv.at[c, 0], mate).wait_recv()
        remote(zland_s.at[c], zland_s.at[c], z_send.at[1], z_recv.at[c, 1], mate).wait_recv()
        figures = jnp.concatenate([zed_s[c]] + [zland_s[c, n] for n in range(NZ - 1)], axis=0)
        peak = jnp.max(figures, axis=0, keepdims=True)
        is_peak = iota((1, ROWS), 1) < SPAN
        factor = jnp.exp2(jnp.where(is_peak, figures - peak, 0.0))
        total = jnp.sum(pltpu.roll(factor, SPAN, 1) * figures, axis=0, keepdims=True)
        here = z * SLICE
        acc = zed[c, z] * to_column(factor[0:1], SLICE, here)
        for n in range(NZ - 1):
            acc += zland[c, n] * to_column(factor[n + 1 : n + 2], SLICE, here)
        top = to_column(peak, SLICE, here)
        tot = to_column(total, SLICE, here + SPAN)
        d_top, d_tot, d_acc = drafted
        joined = jnp.maximum(top, d_top)
        fa, fb = jnp.exp2(top - joined), jnp.exp2(d_top - joined)
        done[c, z] = (acc * fa + d_acc * fb) / (tot * fa + d_tot * fb)

    def regather(c):
        return [
            remote(done.at[c, z], done.at[c, z], g_send.at[0], g_recv.at[c], along_z(dz)) for dz in range(1, NZ)
        ]

    def regathered(c):
        remote(zland.at[c], zland.at[c], g_send.at[0], g_recv.at[c], mate).wait_recv()

    def deliver(c):
        rows = pl.ds(pl.multiple_of(mine * PIECE, PIECE), PIECE)
        part = out_ref.at[seqs(c), rows]
        return [
            remote(part, part, o_send.at[0], o_recv.at[c], in_plane(dx, dy)) for dx, dy in NEAR
        ]

    def delivered(c):
        part = out_ref.at[seqs(c), pl.ds(0, PIECE * len(NEAR))]
        remote(part, part, o_send.at[0], o_recv.at[c], mate).wait_recv()

    def all_sent(ref, sem):
        remote(ref, ref, sem, sem, mate).wait_send()

    def start(copies):
        for copy in copies:
            copy.start()

    pl.semaphore_wait(barrier, len(peers))
    for c in range(CHUNKS):
        for side in range(2):
            ask_far(c, side).start()
    for c in range(CHUNKS):
        ask_mate(c).start()

    small[0].wait()

    def near_own(c, carry):
        for copy in load(c):
            copy.wait()
        attend(0, c, own, own_s, 0)
        return carry

    def near_mate(c, carry):
        ask_mate(c).wait_recv()
        attend(1, c, give, give_s, 0)
        start(swap(0, c))
        return carry

    def near_merge(c, carry):
        merge_cores(0, c)
        start(scatter(0, c))
        return carry

    def far_own(c):
        await_far(c)
        pass_on(c).start()
        attend(2, c, own, own_s, 1)

    def far_mate(c):
        pass_on(c).wait_recv()
        attend(3, c, give, give_s, 1)
        start(swap(1, c))

    def far_merge(c):
        merge_cores(1, c)
        start(scatter(1, c))

    lax.fori_loop(0, CHUNKS, near_own, 0)
    lax.fori_loop(0, CHUNKS, near_mate, 0)
    lax.fori_loop(0, CHUNKS, near_merge, 0)

    def far(c, carry):
        far_own(c)
        far_mate(c)
        return carry

    def far2(c, carry):
        far_merge(c)
        return carry

    lax.fori_loop(0, CHUNKS, far, 0)
    lax.fori_loop(0, CHUNKS, far2, 0)

    all_sent(Q.at[0], q_send.at[0])
    all_sent(Q.at[0], q_send.at[1])
    all_sent(Q.at[0], q_send.at[2])
    all_sent(give, c_send.at[0])
    all_sent(give_s, c_send.at[1])
    for copy in small[1:]:
        copy.wait()
    drafted = [draft(c) for c in range(CHUNKS)]

    for c in range(CHUNKS):
        merge_plane(c)
        start(spread(c))
    for c in range(CHUNKS):
        finish(c, drafted[c])
        start(regather(c))
    all_sent(land, a_send.at[0])
    all_sent(land_s, a_send.at[1])
    all_sent(zland, z_send.at[0])
    all_sent(zland_s, z_send.at[1])
    for c in range(CHUNKS):
        regathered(c)
        rows = pl.ds(pl.multiple_of(mine * PIECE, PIECE), PIECE)
        out_ref[seqs(c), rows] = done[c].reshape(PER, PIECE, WIDTH).astype(BF16)
        start(deliver(c))

    all_sent(zland, g_send.at[0])
    for c in range(CHUNKS):
        delivered(c)
    all_sent(out_ref.at[:, pl.ds(0, PIECE * len(NEAR))], o_send.at[0])


def local(queries, cache_keys, cache_values, draft_keys, draft_values, tree_mask, valid_length):
    dma = pltpu.SemaphoreType.DMA
    n = len(PLANE)
    scratch = [
        pltpu.VMEM((4, SEQS, ROWS, WIDTH), BF16),
        pltpu.VMEM((SEQS, KEYS, WIDTH), BF16),
        pltpu.VMEM((SEQS, KEYS, WIDTH), BF16),
        pltpu.VMEM((SEQS, DRAFT, WIDTH), BF16),
        pltpu.VMEM((SEQS, DRAFT, WIDTH), BF16),
        pltpu.VMEM((SEQS, DRAFT, DRAFT), jnp.int32),
        pltpu.SMEM((SEQS,), jnp.int32),
        pltpu.VMEM((2, SEQS, ROWS, WIDTH), F32),
        pltpu.VMEM((2, CHUNKS, 8, ROWS), F32),
        pltpu.VMEM((2, SEQS, ROWS, WIDTH), BF16),
        pltpu.VMEM((2, CHUNKS, 8, ROWS), F32),
        pltpu.VMEM((2, SEQS, ROWS, WIDTH), BF16),
        pltpu.VMEM((2, CHUNKS, 8, ROWS), F32),
        pltpu.VMEM((2, SEQS, ROWS, WIDTH), BF16),
        pltpu.VMEM((2, CHUNKS, 8, 1, ROWS), F32),
        pltpu.VMEM((CHUNKS, n, PER, PIECE, WIDTH), BF16),
        pltpu.VMEM((CHUNKS, n, 1, ROWS), F32),
        pltpu.VMEM((CHUNKS, NZ, SLICE, WIDTH), F32),
        pltpu.VMEM((CHUNKS, 1, ROWS), F32),
        pltpu.VMEM((CHUNKS, NZ - 1, SLICE, WIDTH), F32),
        pltpu.VMEM((CHUNKS, NZ - 1, 1, ROWS), F32),
        pltpu.VMEM((CHUNKS, NZ, SLICE, WIDTH), F32),
        dma((CHUNKS, 3)),
        dma((4,)),
        dma((3,)),
        dma((3, CHUNKS)),
        dma((2,)),
        dma((2, CHUNKS, 2)),
        dma((2,)),
        dma((CHUNKS, 2)),
        dma((2,)),
        dma((CHUNKS, 2)),
        dma((1,)),
        dma((CHUNKS,)),
        dma((1,)),
        dma((CHUNKS,)),
    ]
    out = pl.pallas_call(
        kernel,
        out_shape=jax.ShapeDtypeStruct((SEQS, ROWS, WIDTH), BF16),
        in_specs=[pl.BlockSpec(memory_space=pltpu.HBM)] * 7,
        out_specs=pl.BlockSpec(memory_space=pltpu.VMEM),
        scratch_shapes=scratch,
        compiler_params=pltpu.CompilerParams(collective_id=0, has_side_effects=True, vmem_limit_bytes=60 << 20),
        name="attend",
    )(
        queries.reshape(SEQS, ROWS, WIDTH),
        cache_keys.reshape(SEQS, KEYS, WIDTH),
        cache_values.reshape(SEQS, KEYS, WIDTH),
        draft_keys.reshape(SEQS, DRAFT, WIDTH),
        draft_values.reshape(SEQS, DRAFT, WIDTH),
        tree_mask,
        valid_length,
    )
    return out.reshape(queries.shape)


def solution(mesh):
    in_specs = (
        P(None, None, "loop", None, None),
        P(None, None, ("loop", "grp"), None),
        P(None, None, ("loop", "grp"), None),
        P(),
        P(),
        P(),
        P(),
    )
    out_specs = P(None, None, "loop", None, None)
    return jax.shard_map(local, mesh=mesh, in_specs=in_specs, out_specs=out_specs, check_vma=False)
```

```python
import math

import jax
import jax.numpy as jnp
from jax import lax
from jax.experimental import pallas as pl
from jax.experimental.pallas import tpu as pltpu
from jax.sharding import PartitionSpec as P

MESH = pl.DeviceIdType.MESH
F32 = jnp.float32
BF16 = jnp.bfloat16

SEQS = 12
ROWS = 128
KEYS = 512
WIDTH = 128
DRAFT = 32
NX, NY, NZ = 4, 4, 8
CHUNKS = 3
PER = SEQS // CHUNKS
PIECE = 16
SPAN = PER * PIECE
NEAR = [(dx, dy) for dy in (0, 2) for dx in range(NX) if (dx, dy) != (0, 0)]
FAR = [(dx, dy) for dx in range(NX) for dy in (1, 3)]

SCALE = math.log2(math.e) / math.sqrt(WIDTH)
FLOOR = -1e30
LOW = -1e29


def iota(shape, axis):
    return lax.broadcasted_iota(jnp.int32, shape, axis)


def to_row(column):
    eye = iota((ROWS, ROWS), 0) == iota((ROWS, ROWS), 1)
    return jnp.sum(jnp.where(eye, column, 0.0), axis=0, keepdims=True)


def to_column(row, rows, first):
    pick = iota((rows, ROWS), 1) == iota((rows, ROWS), 0) + first
    return jnp.sum(jnp.where(pick, row, 0.0), axis=1, keepdims=True)


def by_piece(tile):
    lane = iota((8, ROWS), 1) // PIECE
    sub = iota((8, ROWS), 0)
    out = jnp.zeros((8, ROWS), F32)
    for d in range(8):
        moved = tile if d == 0 else pltpu.roll(tile, PIECE * d, 1)
        diagonal = jnp.sum(jnp.where(lane == sub, moved, 0.0), axis=0, keepdims=True)
        out = jnp.where((lane - sub + 8) % 8 == d, diagonal, out)
    return out


def kernel(
    q_hbm, k_hbm, v_hbm, dk_hbm, dv_hbm, tm_hbm, vl_hbm, out_ref,
    Q, K, V, DK, DV, TM, VL,
    plane, plane_s, xland, xland_s, half_sum, half_s, land, land_s,
    zed, zed_s, zland, zland_s, drafted, drafted_s,
    ld, ld_small, q_send, q_recv, c_send, c_recv, n_send, n_recv, a_send, a_recv, z_send, z_recv, g_send, g_recv, o_send, o_recv,
):
    loop_index = lax.axis_index("loop")
    group_index = lax.axis_index("grp")
    core = loop_index % 2
    x = group_index % NX
    z = (group_index // NX) % NZ
    y = (group_index // (NX * NZ)) * 2 + loop_index // 2

    def device(px, py, pz, pc):
        return ((py % 2) * 2 + pc, ((py // 2) * NZ + pz) * NX + px)

    mate = device(x, y, z, 1 - core)

    def in_plane(dx, dy):
        return device((x + dx) % NX, (y + dy) % NY, z, core)

    def piece_of(px, py):
        return px * 2 + py // 2

    mine = piece_of(x, y)

    def remote(src, dst, send, recv, target):
        return pltpu.make_async_remote_copy(
            src_ref=src, dst_ref=dst, send_sem=send, recv_sem=recv, device_id=target, device_id_type=MESH
        )

    lead = z == 0
    peers = [mate, in_plane(0, 1), in_plane(0, 3)]
    peers += [in_plane(dx, dy) for dx, dy in FAR + NEAR if (dx, dy % 2) != (0, 1)]
    others = [device(x, y, other, core) for other in (1, 7, 2, 6, 3, 5, 4)]
    leader = device(x, y, 0, core)
    barrier = pltpu.get_barrier_semaphore()

    def greet(targets):
        for target in targets:
            pl.semaphore_signal(barrier, inc=1, device_id=target, device_id_type=MESH)

    greet(peers)
    pl.when(lead)(lambda: greet(others))
    pl.when(jnp.logical_not(lead))(lambda: greet([leader]))

    def seqs(c):
        return pl.ds(c * PER, PER)

    def load(c):
        return [
            pltpu.make_async_copy(q_hbm.at[seqs(c)], Q.at[0, seqs(c)], ld.at[c, 0]),
            pltpu.make_async_copy(k_hbm.at[seqs(c)], K.at[seqs(c), 0], ld.at[c, 1]),
            pltpu.make_async_copy(v_hbm.at[seqs(c)], V.at[seqs(c), 0], ld.at[c, 2]),
        ]

    small = [
        pltpu.make_async_copy(vl_hbm, VL, ld_small.at[0]),
        pltpu.make_async_copy(dk_hbm, DK, ld_small.at[1]),
        pltpu.make_async_copy(dv_hbm, DV, ld_small.at[2]),
        pltpu.make_async_copy(tm_hbm, TM, ld_small.at[3]),
    ]
    small[0].start()
    for c in range(CHUNKS):
        for copy in load(c):
            copy.start()
    for copy in small[1:]:
        copy.start()

    half = ROWS // 2

    def to_mate(c):
        return [
            remote(k_hbm.at[seqs(c)], K.at[seqs(c), 1], c_send.at[0], c_recv.at[c, 0], mate),
            remote(v_hbm.at[seqs(c)], V.at[seqs(c), 1], c_send.at[1], c_recv.at[c, 1], mate),
        ]

    def ask_far(c, side):
        rows = pl.ds(side * half, half)
        return remote(
            q_hbm.at[seqs(c), rows], Q.at[1, seqs(c), rows], q_send.at[0], q_recv.at[c],
            in_plane(0, 1 if side == 0 else 3),
        )

    def await_far(c):
        remote(Q.at[1, seqs(c)], Q.at[1, seqs(c)], q_send.at[0], q_recv.at[c], mate).wait_recv()

    def first(member):
        return (member * (NX * 2 * NZ) + group_index) * KEYS

    lane = iota((1, 2 * KEYS), 1)
    position = jnp.where(lane < KEYS, first(loop_index), first(loop_index + 1 - 2 * core) - KEYS) + lane
    ones = jnp.ones((2 * KEYS, WIDTH), BF16)
    sub8 = iota((8, ROWS), 0)

    def attend(side, c):
        def one(i, tile):
            s = c * PER + i
            scores = lax.dot_general(Q[side, s], K[s].reshape(2 * KEYS, WIDTH), (((1,), (1,)), ((), ())), preferred_element_type=F32)
            scores = jnp.where(position < VL[s], scores * SCALE, FLOOR)
            peak = jnp.maximum(jnp.max(scores, axis=1, keepdims=True), LOW)
            weights = jnp.exp2(scores - peak).astype(BF16)
            values = jnp.concatenate([V[s].reshape(2 * KEYS, WIDTH), ones], axis=1)
            both = jnp.dot(weights, values, preferred_element_type=F32)
            plane[side, s] = both[:, :WIDTH].astype(BF16)
            tile = jnp.where(sub8 == i, to_row(peak), tile)
            return jnp.where(sub8 == PER + i, to_row(both[:, WIDTH:]), tile)

        pieces = by_piece(lax.fori_loop(0, PER, one, jnp.zeros((8, ROWS), F32), unroll=PER))
        for p in range(8):
            plane_s[side, c, p] = pieces[p : p + 1]

    def piece_rows(piece, count=1):
        return pl.ds(pl.multiple_of(piece * PIECE, PIECE), count * PIECE)

    def scatter_x(c):
        copies = []
        for dx in range(1, NX):
            pair = ((x + dx) % NX) * 2
            target = in_plane(dx, 0)
            copies.append(
                remote(plane.at[0, seqs(c), piece_rows(pair, 2)], xland.at[c, dx - 1], n_send.at[0], n_recv.at[c, 0], target)
            )
            copies.append(
                remote(plane_s.at[0, c, pl.ds(pair, 2)], xland_s.at[c, dx - 1], n_send.at[1], n_recv.at[c, 1], target)
            )
        return copies

    def scatter_far(c):
        copies = []
        for n, (dx, dy) in enumerate(FAR):
            piece = piece_of((x + dx) % NX, (y + dy) % NY)
            target = in_plane(dx, dy)
            copies.append(remote(plane.at[1, seqs(c), piece_rows(piece)], land.at[c, n], a_send.at[0], a_recv.at[c, 0], target))
            copies.append(remote(plane_s.at[1, c, piece], land_s.at[c, n], a_send.at[1], a_recv.at[c, 1], target))
        return copies

    def across(c):
        n, target = len(FAR), in_plane(0, 2)
        return [
            remote(half_sum.at[c], land.at[c, n], a_send.at[0], a_recv.at[c, 0], target),
            remote(half_s.at[c], land_s.at[c, n], a_send.at[1], a_recv.at[c, 1], target),
        ]

    def merge(figures, parts):
        peak = jnp.max(figures, axis=0, keepdims=True)
        is_peak = iota((1, ROWS), 1) < SPAN
        factor = jnp.exp2(jnp.where(is_peak, figures - peak, 0.0))
        total = jnp.sum(pltpu.roll(factor, SPAN, 1) * figures, axis=0, keepdims=True)
        acc = jnp.zeros((SPAN, WIDTH), F32)
        for n, part in enumerate(parts):
            acc += part.reshape(SPAN, WIDTH).astype(F32) * to_column(factor[n : n + 1], SPAN, 0)
        return jnp.where(is_peak, peak, total), acc

    def near_sources(c, level):
        piece = x * 2 + level
        rows = pl.ds(pl.multiple_of(level * PIECE, PIECE), PIECE)
        figures = [plane_s[0, c, piece]] + [xland_s[c, n, level] for n in range(NX - 1)]
        parts = [plane[0, seqs(c), piece_rows(piece)]] + [xland[c, n, :, rows] for n in range(NX - 1)]
        return figures, parts

    def merge_across(c):
        remote(xland.at[c], xland.at[c], n_send.at[0], n_recv.at[c, 0], mate).wait_recv()
        remote(xland_s.at[c], xland_s.at[c], n_send.at[1], n_recv.at[c, 1], mate).wait_recv()
        figures, parts = near_sources(c, 1 - y // 2)
        row, acc = merge(jnp.concatenate(figures, axis=0), parts)
        half_s[c] = row
        half_sum[c] = acc.reshape(PER, PIECE, WIDTH).astype(BF16)
        start(across(c))

    def merge_plane(c):
        remote(land.at[c], land.at[c], a_send.at[0], a_recv.at[c, 0], mate).wait_recv()
        remote(land_s.at[c], land_s.at[c], a_send.at[1], a_recv.at[c, 1], mate).wait_recv()
        figures, parts = near_sources(c, y // 2)
        figures += [land_s[c, n] for n in range(len(FAR) + 1)]
        parts += [land[c, n] for n in range(len(FAR) + 1)]
        row, acc = merge(jnp.concatenate(figures, axis=0), parts)
        zed_s[c] = row
        zed[c] = acc.reshape(PER, PIECE, WIDTH).astype(BF16)

    def to_leader(c):
        return [
            remote(zed.at[c], zland.at[c, z - 1], z_send.at[0], z_recv.at[c, 0], leader),
            remote(zed_s.at[c], zland_s.at[c, z - 1], z_send.at[1], z_recv.at[c, 1], leader),
        ]

    def draft(c):
        allowed_rows = pl.ds(pl.multiple_of((mine % 2) * PIECE, PIECE), PIECE)
        for i in range(PER):
            s = c * PER + i
            queries = Q[0, s, piece_rows(mine)]
            scores = lax.dot_general(queries, DK[s], (((1,), (1,)), ((), ())), preferred_element_type=F32) * SCALE
            allowed = TM[s, allowed_rows] == 1
            peak = jnp.max(jnp.where(allowed, scores, FLOOR), axis=1, keepdims=True)
            weights = jnp.where(allowed, jnp.exp2(scores - peak), 0.0).astype(BF16)
            total = jnp.sum(weights.astype(F32), axis=1, keepdims=True)
            rows = pl.ds(i * PIECE, PIECE)
            drafted[c, rows] = jnp.dot(weights, DV[s], preferred_element_type=F32)
            drafted_s[c, 0, rows] = jnp.broadcast_to(peak, (PIECE, WIDTH))
            drafted_s[c, 1, rows] = jnp.broadcast_to(total, (PIECE, WIDTH))

    def finish(c):
        remote(zland.at[c], zland.at[c], z_send.at[0], z_recv.at[c, 0], mate).wait_recv()
        remote(zland_s.at[c], zland_s.at[c], z_send.at[1], z_recv.at[c, 1], mate).wait_recv()
        figures = jnp.concatenate([zed_s[c]] + [zland_s[c, n] for n in range(NZ - 1)], axis=0)
        row, acc = merge(figures, [zed[c]] + [zland[c, n] for n in range(NZ - 1)])
        top, total = to_column(row, SPAN, 0), to_column(row, SPAN, SPAN)
        joined = jnp.maximum(top, drafted_s[c, 0])
        fa, fb = jnp.exp2(top - joined), jnp.exp2(drafted_s[c, 0] - joined)
        result = (acc * fa + drafted[c] * fb) / (total * fa + drafted_s[c, 1] * fb)
        out_ref[seqs(c), piece_rows(mine)] = result.reshape(PER, PIECE, WIDTH).astype(BF16)

    def from_leader(c, targets):
        part = out_ref.at[seqs(c), piece_rows(mine)]
        return [remote(part, part, g_send.at[0], g_recv.at[c], target) for target in targets]

    def deliver(c):
        rows = pl.ds(pl.multiple_of(mine * PIECE, PIECE), PIECE)
        part = out_ref.at[seqs(c), rows]
        return [
            remote(part, part, o_send.at[0], o_recv.at[c], in_plane(dx, dy)) for dx, dy in NEAR
        ]

    def delivered(c):
        part = out_ref.at[seqs(c), pl.ds(0, PIECE * len(NEAR))]
        remote(part, part, o_send.at[0], o_recv.at[c], mate).wait_recv()

    def all_sent(ref, sem):
        remote(ref, ref, sem, sem, mate).wait_send()

    def start(copies):
        for copy in copies:
            copy.start()

    pl.semaphore_wait(barrier, len(peers) + jnp.where(lead, NZ - 1, 1))
    for c in range(CHUNKS):
        for side in range(2):
            ask_far(c, side).start()
    for c in range(CHUNKS):
        start(to_mate(c))

    small[0].wait()

    def near(c, carry):
        for copy in load(c):
            copy.wait()
        for copy in to_mate(c):
            copy.wait_recv()
        attend(0, c)
        start(scatter_x(c))
        return carry

    def far(c):
        await_far(c)
        attend(1, c)
        start(scatter_far(c))

    lax.fori_loop(0, CHUNKS, near, 0)

    def step(i, carry):
        pl.when(i < CHUNKS)(lambda: far(i))
        pl.when(i >= 1)(lambda: merge_across(i - 1))
        return carry

    lax.fori_loop(0, CHUNKS + 1, step, 0)

    all_sent(Q.at[0], q_send.at[0])
    all_sent(K.at[:, 0], c_send.at[0])
    all_sent(V.at[:, 0], c_send.at[1])
    for copy in small[1:]:
        copy.wait()

    @pl.when(lead)
    def _():
        for c in range(CHUNKS):
            draft(c)

    for c in range(CHUNKS):
        merge_plane(c)

        @pl.when(jnp.logical_not(lead))
        def _():
            start(to_leader(c))

    all_sent(xland, n_send.at[0])
    all_sent(xland_s, n_send.at[1])
    all_sent(land, a_send.at[0])
    all_sent(land_s, a_send.at[1])

    for c in range(CHUNKS):

        @pl.when(lead)
        def _():
            finish(c)
            start(from_leader(c, others))

        @pl.when(jnp.logical_not(lead))
        def _():
            from_leader(c, [leader])[0].wait_recv()

        start(deliver(c))

    @pl.when(lead)
    def _():
        part = out_ref.at[:, pl.ds(0, PIECE * (NZ - 1))]
        all_sent(part, g_send.at[0])

    @pl.when(jnp.logical_not(lead))
    def _():
        all_sent(zed, z_send.at[0])
        all_sent(zed_s, z_send.at[1])

    for c in range(CHUNKS):
        delivered(c)
    all_sent(out_ref.at[:, pl.ds(0, PIECE * len(NEAR))], o_send.at[0])


def local(queries, cache_keys, cache_values, draft_keys, draft_values, tree_mask, valid_length):
    dma = pltpu.SemaphoreType.DMA
    n = len(FAR) + 1
    scratch = [
        pltpu.VMEM((2, SEQS, ROWS, WIDTH), BF16),
        pltpu.VMEM((SEQS, 2, KEYS, WIDTH), BF16),
        pltpu.VMEM((SEQS, 2, KEYS, WIDTH), BF16),
        pltpu.VMEM((SEQS, DRAFT, WIDTH), BF16),
        pltpu.VMEM((SEQS, DRAFT, WIDTH), BF16),
        pltpu.VMEM((SEQS, DRAFT, DRAFT), jnp.int32),
        pltpu.SMEM((SEQS,), jnp.int32),
        pltpu.VMEM((2, SEQS, ROWS, WIDTH), BF16),
        pltpu.VMEM((2, CHUNKS, 8, 1, ROWS), F32),
        pltpu.VMEM((CHUNKS, NX - 1, PER, 2 * PIECE, WIDTH), BF16),
        pltpu.VMEM((CHUNKS, NX - 1, 2, 1, ROWS), F32),
        pltpu.VMEM((CHUNKS, PER, PIECE, WIDTH), BF16),
        pltpu.VMEM((CHUNKS, 1, ROWS), F32),
        pltpu.VMEM((CHUNKS, n, PER, PIECE, WIDTH), BF16),
        pltpu.VMEM((CHUNKS, n, 1, ROWS), F32),
        pltpu.VMEM((CHUNKS, PER, PIECE, WIDTH), BF16),
        pltpu.VMEM((CHUNKS, 1, ROWS), F32),
        pltpu.VMEM((CHUNKS, NZ - 1, PER, PIECE, WIDTH), BF16),
        pltpu.VMEM((CHUNKS, NZ - 1, 1, ROWS), F32),
        pltpu.VMEM((CHUNKS, SPAN, WIDTH), F32),
        pltpu.VMEM((CHUNKS, 2, SPAN, WIDTH), F32),
        dma((CHUNKS, 3)),
        dma((4,)),
        dma((1,)),
        dma((CHUNKS,)),
        dma((2,)),
        dma((CHUNKS, 2)),
        dma((2,)),
        dma((CHUNKS, 2)),
        dma((2,)),
        dma((CHUNKS, 2)),
        dma((2,)),
        dma((CHUNKS, 2)),
        dma((1,)),
        dma((CHUNKS,)),
        dma((1,)),
        dma((CHUNKS,)),
    ]
    out = pl.pallas_call(
        kernel,
        out_shape=jax.ShapeDtypeStruct((SEQS, ROWS, WIDTH), BF16),
        in_specs=[pl.BlockSpec(memory_space=pltpu.HBM)] * 7,
        out_specs=pl.BlockSpec(memory_space=pltpu.VMEM),
        scratch_shapes=scratch,
        compiler_params=pltpu.CompilerParams(collective_id=0, has_side_effects=True, vmem_limit_bytes=60 << 20),
        name="attend",
    )(
        queries.reshape(SEQS, ROWS, WIDTH),
        cache_keys.reshape(SEQS, KEYS, WIDTH),
        cache_values.reshape(SEQS, KEYS, WIDTH),
        draft_keys.reshape(SEQS, DRAFT, WIDTH),
        draft_values.reshape(SEQS, DRAFT, WIDTH),
        tree_mask,
        valid_length,
    )
    return out.reshape(queries.shape)


def solution(mesh):
    in_specs = (
        P(None, None, "loop", None, None),
        P(None, None, ("loop", "grp"), None),
        P(None, None, ("loop", "grp"), None),
        P(),
        P(),
        P(),
        P(),
    )
    out_specs = P(None, None, "loop", None, None)
    return jax.shard_map(local, mesh=mesh, in_specs=in_specs, out_specs=out_specs, check_vma=False)
```

```python
import math

import jax
import jax.numpy as jnp
from jax import lax
from jax.experimental import pallas as pl
from jax.experimental.pallas import tpu as pltpu
from jax.sharding import PartitionSpec as P

MESH = pl.DeviceIdType.MESH
F32 = jnp.float32
BF16 = jnp.bfloat16

SEQS = 12
ROWS = 128
KEYS = 512
WIDTH = 128
DRAFT = 32
NX, NY, NZ = 4, 4, 8
CHUNKS = 3
PER = SEQS // CHUNKS
PIECE = 16
SPAN = PER * PIECE
NEAR = [(dx, dy) for dy in (0, 2) for dx in range(NX) if (dx, dy) != (0, 0)]
FAR = [(dx, dy) for dx in range(NX) for dy in (1, 3)]

SCALE = math.log2(math.e) / math.sqrt(WIDTH)
FLOOR = -1e30
LOW = -1e29


def iota(shape, axis):
    return lax.broadcasted_iota(jnp.int32, shape, axis)


def to_row(column):
    eye = iota((ROWS, ROWS), 0) == iota((ROWS, ROWS), 1)
    return jnp.sum(jnp.where(eye, column, 0.0), axis=0, keepdims=True)


def to_column(row, rows, first):
    pick = iota((rows, ROWS), 1) == iota((rows, ROWS), 0) + first
    return jnp.sum(jnp.where(pick, row, 0.0), axis=1, keepdims=True)


def by_piece(tile):
    lane = iota((8, ROWS), 1) // PIECE
    sub = iota((8, ROWS), 0)
    out = jnp.zeros((8, ROWS), F32)
    for d in range(8):
        moved = tile if d == 0 else pltpu.roll(tile, PIECE * d, 1)
        diagonal = jnp.sum(jnp.where(lane == sub, moved, 0.0), axis=0, keepdims=True)
        out = jnp.where((lane - sub + 8) % 8 == d, diagonal, out)
    return out


def kernel(
    q_hbm, k_hbm, v_hbm, dk_hbm, dv_hbm, tm_hbm, vl_hbm, out_ref,
    Q, K, V, DK, DV, TM, VL,
    plane, plane_s, xland, xland_s, half_sum, half_s, land, land_s,
    zed, zed_s, zland, zland_s, drafted, drafted_s, final,
    ld, ld_small, q_send, q_recv, c_send, c_recv, n_send, n_recv, a_send, a_recv, z_send, z_recv, g_send, g_recv, o_send, o_recv,
):
    loop_index = lax.axis_index("loop")
    group_index = lax.axis_index("grp")
    core = loop_index % 2
    x = group_index % NX
    z = (group_index // NX) % NZ
    y = (group_index // (NX * NZ)) * 2 + loop_index // 2

    def device(px, py, pz, pc):
        return ((py % 2) * 2 + pc, ((py // 2) * NZ + pz) * NX + px)

    mate = device(x, y, z, 1 - core)

    def in_plane(dx, dy):
        return device((x + dx) % NX, (y + dy) % NY, z, core)

    def piece_of(px, py):
        return px * 2 + py // 2

    mine = piece_of(x, y)

    def remote(src, dst, send, recv, target):
        return pltpu.make_async_remote_copy(
            src_ref=src, dst_ref=dst, send_sem=send, recv_sem=recv, device_id=target, device_id_type=MESH
        )

    lead = z == 0
    peers = [mate, in_plane(0, 1), in_plane(0, 3)]
    peers += [in_plane(dx, dy) for dx, dy in FAR + NEAR if (dx, dy % 2) != (0, 1)]
    others = [device(x, y, other, core) for other in (1, 7, 2, 6, 3, 5, 4)]
    leader = device(x, y, 0, core)
    barrier = pltpu.get_barrier_semaphore()

    def greet(targets):
        for target in targets:
            pl.semaphore_signal(barrier, inc=1, device_id=target, device_id_type=MESH)

    greet(peers)
    pl.when(lead)(lambda: greet(others))
    pl.when(jnp.logical_not(lead))(lambda: greet([leader]))

    def seqs(c):
        return pl.ds(c * PER, PER)

    def load(c):
        return [
            pltpu.make_async_copy(q_hbm.at[seqs(c)], Q.at[0, seqs(c)], ld.at[c, 0]),
            pltpu.make_async_copy(k_hbm.at[seqs(c)], K.at[seqs(c), 0], ld.at[c, 1]),
            pltpu.make_async_copy(v_hbm.at[seqs(c)], V.at[seqs(c), 0], ld.at[c, 2]),
        ]

    small = [
        pltpu.make_async_copy(vl_hbm, VL, ld_small.at[0]),
        pltpu.make_async_copy(dk_hbm, DK, ld_small.at[1]),
        pltpu.make_async_copy(dv_hbm, DV, ld_small.at[2]),
        pltpu.make_async_copy(tm_hbm, TM, ld_small.at[3]),
    ]
    small[0].start()
    for c in range(CHUNKS):
        for copy in load(c):
            copy.start()
    for copy in small[1:]:
        copy.start()

    half = ROWS // 2

    def to_mate(c):
        return [
            remote(k_hbm.at[seqs(c)], K.at[seqs(c), 1], c_send.at[0], c_recv.at[c, 0], mate),
            remote(v_hbm.at[seqs(c)], V.at[seqs(c), 1], c_send.at[1], c_recv.at[c, 1], mate),
        ]

    def ask_far(c, side):
        rows = pl.ds(side * half, half)
        return remote(
            q_hbm.at[seqs(c), rows], Q.at[1, seqs(c), rows], q_send.at[0], q_recv.at[c],
            in_plane(0, 1 if side == 0 else 3),
        )

    def await_far(c):
        remote(Q.at[1, seqs(c)], Q.at[1, seqs(c)], q_send.at[0], q_recv.at[c], mate).wait_recv()

    def first(member):
        return (member * (NX * 2 * NZ) + group_index) * KEYS

    lane = iota((1, 2 * KEYS), 1)
    position = jnp.where(lane < KEYS, first(loop_index), first(loop_index + 1 - 2 * core) - KEYS) + lane
    ones = jnp.ones((2 * KEYS, WIDTH), BF16)
    sub8 = iota((8, ROWS), 0)

    def attend(sides, c):
        def one(i, tiles):
            s = c * PER + i
            values = jnp.concatenate([V[s].reshape(2 * KEYS, WIDTH), ones], axis=1)
            out = []
            for side, tile in zip(sides, tiles):
                scores = lax.dot_general(
                    Q[side, s], K[s].reshape(2 * KEYS, WIDTH), (((1,), (1,)), ((), ())), preferred_element_type=F32
                )
                scores = jnp.where(position < VL[s], scores * SCALE, FLOOR)
                peak = jnp.maximum(jnp.max(scores, axis=1, keepdims=True), LOW)
                weights = jnp.exp2(scores - peak).astype(BF16)
                both = jnp.dot(weights, values, preferred_element_type=F32)
                plane[side, s] = both[:, :WIDTH].astype(BF16)
                tile = jnp.where(sub8 == i, to_row(peak), tile)
                out.append(jnp.where(sub8 == PER + i, to_row(both[:, WIDTH:]), tile))
            return tuple(out)

        tiles = lax.fori_loop(0, PER, one, (jnp.zeros((8, ROWS), F32),) * len(sides), unroll=PER)
        for side, tile in zip(sides, tiles):
            pieces = by_piece(tile)
            for p in range(8):
                plane_s[side, c, p] = pieces[p : p + 1]

    def piece_rows(piece, count=1):
        return pl.ds(pl.multiple_of(piece * PIECE, PIECE), count * PIECE)

    def scatter_x(c):
        copies = []
        for dx in range(1, NX):
            pair = ((x + dx) % NX) * 2
            target = in_plane(dx, 0)
            copies.append(
                remote(plane.at[0, seqs(c), piece_rows(pair, 2)], xland.at[c, dx - 1], n_send.at[0], n_recv.at[c, 0], target)
            )
            copies.append(
                remote(plane_s.at[0, c, pl.ds(pair, 2)], xland_s.at[c, dx - 1], n_send.at[1], n_recv.at[c, 1], target)
            )
        return copies

    def scatter_far(c):
        copies = []
        for n, (dx, dy) in enumerate(FAR):
            piece = piece_of((x + dx) % NX, (y + dy) % NY)
            target = in_plane(dx, dy)
            copies.append(remote(plane.at[1, seqs(c), piece_rows(piece)], land.at[c, n], a_send.at[0], a_recv.at[c, 0], target))
            copies.append(remote(plane_s.at[1, c, piece], land_s.at[c, n], a_send.at[1], a_recv.at[c, 1], target))
        return copies

    def across(c):
        n, target = len(FAR), in_plane(0, 2)
        return [
            remote(half_sum.at[c], land.at[c, n], a_send.at[0], a_recv.at[c, 0], target),
            remote(half_s.at[c], land_s.at[c, n], a_send.at[1], a_recv.at[c, 1], target),
        ]

    def merge(figures, parts):
        peak = jnp.max(figures, axis=0, keepdims=True)
        is_peak = iota((1, ROWS), 1) < SPAN
        factor = jnp.exp2(jnp.where(is_peak, figures - peak, 0.0))
        total = jnp.sum(pltpu.roll(factor, SPAN, 1) * figures, axis=0, keepdims=True)
        acc = jnp.zeros((SPAN, WIDTH), F32)
        for n, part in enumerate(parts):
            acc += part.reshape(SPAN, WIDTH).astype(F32) * to_column(factor[n : n + 1], SPAN, 0)
        return jnp.where(is_peak, peak, total), acc

    def near_sources(c, level):
        piece = x * 2 + level
        rows = pl.ds(pl.multiple_of(level * PIECE, PIECE), PIECE)
        figures = [plane_s[0, c, piece]] + [xland_s[c, n, level] for n in range(NX - 1)]
        parts = [plane[0, seqs(c), piece_rows(piece)]] + [xland[c, n, :, rows] for n in range(NX - 1)]
        return figures, parts

    def merge_across(c):
        remote(xland.at[c], xland.at[c], n_send.at[0], n_recv.at[c, 0], mate).wait_recv()
        remote(xland_s.at[c], xland_s.at[c], n_send.at[1], n_recv.at[c, 1], mate).wait_recv()
        figures, parts = near_sources(c, 1 - y // 2)
        row, acc = merge(jnp.concatenate(figures, axis=0), parts)
        half_s[c] = row
        half_sum[c] = acc.reshape(PER, PIECE, WIDTH).astype(BF16)
        start(across(c))

    def merge_plane(c):
        remote(land.at[c], land.at[c], a_send.at[0], a_recv.at[c, 0], mate).wait_recv()
        remote(land_s.at[c], land_s.at[c], a_send.at[1], a_recv.at[c, 1], mate).wait_recv()
        figures, parts = near_sources(c, y // 2)
        figures += [land_s[c, n] for n in range(len(FAR) + 1)]
        parts += [land[c, n] for n in range(len(FAR) + 1)]
        row, acc = merge(jnp.concatenate(figures, axis=0), parts)
        zed_s[c] = row
        zed[c] = acc.reshape(PER, PIECE, WIDTH).astype(BF16)

    def to_leader(c):
        return [
            remote(zed.at[c], zland.at[c, z - 1], z_send.at[0], z_recv.at[c, 0], leader),
            remote(zed_s.at[c], zland_s.at[c, z - 1], z_send.at[1], z_recv.at[c, 1], leader),
        ]

    def draft(c):
        allowed_rows = pl.ds(pl.multiple_of((mine % 2) * PIECE, PIECE), PIECE)
        for i in range(PER):
            s = c * PER + i
            queries = Q[0, s, piece_rows(mine)]
            scores = lax.dot_general(queries, DK[s], (((1,), (1,)), ((), ())), preferred_element_type=F32) * SCALE
            allowed = TM[s, allowed_rows] == 1
            peak = jnp.max(jnp.where(allowed, scores, FLOOR), axis=1, keepdims=True)
            weights = jnp.where(allowed, jnp.exp2(scores - peak), 0.0).astype(BF16)
            total = jnp.sum(weights.astype(F32), axis=1, keepdims=True)
            rows = pl.ds(i * PIECE, PIECE)
            drafted[c, rows] = jnp.dot(weights, DV[s], preferred_element_type=F32)
            drafted_s[c, 0, rows] = jnp.broadcast_to(peak, (PIECE, WIDTH))
            drafted_s[c, 1, rows] = jnp.broadcast_to(total, (PIECE, WIDTH))

    def finish(c):
        remote(zland.at[c], zland.at[c], z_send.at[0], z_recv.at[c, 0], mate).wait_recv()
        remote(zland_s.at[c], zland_s.at[c], z_send.at[1], z_recv.at[c, 1], mate).wait_recv()
        figures = jnp.concatenate([zed_s[c]] + [zland_s[c, n] for n in range(NZ - 1)], axis=0)
        row, acc = merge(figures, [zed[c]] + [zland[c, n] for n in range(NZ - 1)])
        top, total = to_column(row, SPAN, 0), to_column(row, SPAN, SPAN)
        joined = jnp.maximum(top, drafted_s[c, 0])
        fa, fb = jnp.exp2(top - joined), jnp.exp2(drafted_s[c, 0] - joined)
        result = (acc * fa + drafted[c] * fb) / (total * fa + drafted_s[c, 1] * fb)
        final[c] = result.reshape(PER, PIECE, WIDTH).astype(BF16)

    def from_leader(c, targets):
        return [remote(final.at[c], final.at[c], g_send.at[0], g_recv.at[c], target) for target in targets]

    def keep(c):
        return pltpu.make_async_copy(final.at[c], out_ref.at[seqs(c), piece_rows(mine)], ld.at[c, 0])

    def deliver(c):
        place = out_ref.at[seqs(c), piece_rows(mine)]
        return [remote(final.at[c], place, o_send.at[0], o_recv.at[c], in_plane(dx, dy)) for dx, dy in NEAR]

    def delivered(c):
        part = out_ref.at[seqs(c), pl.ds(0, PIECE * len(NEAR))]
        remote(part, part, o_send.at[0], o_recv.at[c], mate).wait_recv()

    def all_sent(ref, sem):
        remote(ref, ref, sem, sem, mate).wait_send()

    def start(copies):
        for copy in copies:
            copy.start()

    pl.semaphore_wait(barrier, len(peers) + jnp.where(lead, NZ - 1, 1))
    for c in range(CHUNKS):
        for side in range(2):
            ask_far(c, side).start()
    for c in range(CHUNKS):
        start(to_mate(c))

    small[0].wait()

    def near(c):
        for copy in load(c):
            copy.wait()
        for copy in to_mate(c):
            copy.wait_recv()
        attend((0,), c)
        start(scatter_x(c))

    def far(c):
        await_far(c)
        attend((1,), c)
        start(scatter_far(c))

    for c in range(CHUNKS):
        near(c)
    far(0)
    far(1)
    merge_across(0)
    far(2)
    merge_across(1)
    merge_across(2)

    all_sent(Q.at[0], q_send.at[0])
    all_sent(K.at[:, 0], c_send.at[0])
    all_sent(V.at[:, 0], c_send.at[1])
    for copy in small[1:]:
        copy.wait()

    @pl.when(lead)
    def _():
        for c in range(CHUNKS):
            draft(c)

    for c in range(CHUNKS):
        merge_plane(c)

        @pl.when(jnp.logical_not(lead))
        def _():
            start(to_leader(c))

    all_sent(xland, n_send.at[0])
    all_sent(xland_s, n_send.at[1])
    all_sent(land, a_send.at[0])
    all_sent(land_s, a_send.at[1])

    for c in range(CHUNKS):

        @pl.when(lead)
        def _():
            finish(c)
            start(from_leader(c, others))

        @pl.when(jnp.logical_not(lead))
        def _():
            from_leader(c, [leader])[0].wait_recv()

        start(deliver(c) + [keep(c)])

    @pl.when(lead)
    def _():
        all_sent(zland, g_send.at[0])

    @pl.when(jnp.logical_not(lead))
    def _():
        all_sent(zed, z_send.at[0])
        all_sent(zed_s, z_send.at[1])

    for c in range(CHUNKS):
        delivered(c)
        keep(c).wait()
    all_sent(zland, o_send.at[0])


def local(queries, cache_keys, cache_values, draft_keys, draft_values, tree_mask, valid_length):
    dma = pltpu.SemaphoreType.DMA
    n = len(FAR) + 1
    scratch = [
        pltpu.VMEM((2, SEQS, ROWS, WIDTH), BF16),
        pltpu.VMEM((SEQS, 2, KEYS, WIDTH), BF16),
        pltpu.VMEM((SEQS, 2, KEYS, WIDTH), BF16),
        pltpu.VMEM((SEQS, DRAFT, WIDTH), BF16),
        pltpu.VMEM((SEQS, DRAFT, WIDTH), BF16),
        pltpu.VMEM((SEQS, DRAFT, DRAFT), jnp.int32),
        pltpu.SMEM((SEQS,), jnp.int32),
        pltpu.VMEM((2, SEQS, ROWS, WIDTH), BF16),
        pltpu.VMEM((2, CHUNKS, 8, 1, ROWS), F32),
        pltpu.VMEM((CHUNKS, NX - 1, PER, 2 * PIECE, WIDTH), BF16),
        pltpu.VMEM((CHUNKS, NX - 1, 2, 1, ROWS), F32),
        pltpu.VMEM((CHUNKS, PER, PIECE, WIDTH), BF16),
        pltpu.VMEM((CHUNKS, 1, ROWS), F32),
        pltpu.VMEM((CHUNKS, n, PER, PIECE, WIDTH), BF16),
        pltpu.VMEM((CHUNKS, n, 1, ROWS), F32),
        pltpu.VMEM((CHUNKS, PER, PIECE, WIDTH), BF16),
        pltpu.VMEM((CHUNKS, 1, ROWS), F32),
        pltpu.VMEM((CHUNKS, NZ - 1, PER, PIECE, WIDTH), BF16),
        pltpu.VMEM((CHUNKS, NZ - 1, 1, ROWS), F32),
        pltpu.VMEM((CHUNKS, SPAN, WIDTH), F32),
        pltpu.VMEM((CHUNKS, 2, SPAN, WIDTH), F32),
        pltpu.VMEM((CHUNKS, PER, PIECE, WIDTH), BF16),
        dma((CHUNKS, 3)),
        dma((4,)),
        dma((1,)),
        dma((CHUNKS,)),
        dma((2,)),
        dma((CHUNKS, 2)),
        dma((2,)),
        dma((CHUNKS, 2)),
        dma((2,)),
        dma((CHUNKS, 2)),
        dma((2,)),
        dma((CHUNKS, 2)),
        dma((1,)),
        dma((CHUNKS,)),
        dma((1,)),
        dma((CHUNKS,)),
    ]
    operands = [
        queries.reshape(SEQS, ROWS, WIDTH),
        cache_keys.reshape(SEQS, KEYS, WIDTH),
        cache_values.reshape(SEQS, KEYS, WIDTH),
        draft_keys.reshape(SEQS, DRAFT, WIDTH),
        draft_values.reshape(SEQS, DRAFT, WIDTH),
        tree_mask,
        valid_length,
    ]
    operands = [pltpu.with_memory_space_constraint(a, pltpu.HBM) for a in operands]
    out = pl.pallas_call(
        kernel,
        out_shape=pltpu.VMEM((SEQS, ROWS, WIDTH), BF16),
        in_specs=[pl.BlockSpec(memory_space=pltpu.HBM)] * 7,
        out_specs=pl.BlockSpec(memory_space=pltpu.VMEM),
        scratch_shapes=scratch,
        compiler_params=pltpu.CompilerParams(collective_id=0, has_side_effects=True, vmem_limit_bytes=40 << 20),
        name="attend",
    )(
        *operands,
    )
    return out.reshape(queries.shape)


def solution(mesh):
    in_specs = (
        P(None, None, "loop", None, None),
        P(None, None, ("loop", "grp"), None),
        P(None, None, ("loop", "grp"), None),
        P(),
        P(),
        P(),
        P(),
    )
    out_specs = P(None, None, "loop", None, None)
    return jax.shard_map(local, mesh=mesh, in_specs=in_specs, out_specs=out_specs, check_vma=False)
```

```python
import math

import jax
import jax.numpy as jnp
from jax import lax
from jax.experimental import pallas as pl
from jax.experimental.pallas import tpu as pltpu
from jax.sharding import PartitionSpec as P

MESH = pl.DeviceIdType.MESH
F32 = jnp.float32
BF16 = jnp.bfloat16

SEQS = 12
ROWS = 128
KEYS = 512
WIDTH = 128
DRAFT = 32
NX, NY, NZ = 4, 4, 8
CHUNKS = 3
PER = SEQS // CHUNKS
PIECE = 16
SPAN = PER * PIECE
NEAR = [(dx, dy) for dy in (0, 2) for dx in range(NX) if (dx, dy) != (0, 0)]
FAR = [(dx, dy) for dx in range(NX) for dy in (1, 3)]

SCALE = math.log2(math.e) / math.sqrt(WIDTH)
FLOOR = -1e30
LOW = -1e29


def iota(shape, axis):
    return lax.broadcasted_iota(jnp.int32, shape, axis)


def to_row(column):
    eye = iota((ROWS, ROWS), 0) == iota((ROWS, ROWS), 1)
    return jnp.sum(jnp.where(eye, column, 0.0), axis=0, keepdims=True)


def to_column(row, rows, first):
    pick = iota((rows, ROWS), 1) == iota((rows, ROWS), 0) + first
    return jnp.sum(jnp.where(pick, row, 0.0), axis=1, keepdims=True)


def by_piece(tile):
    lane = iota((8, ROWS), 1) // PIECE
    sub = iota((8, ROWS), 0)
    out = jnp.zeros((8, ROWS), F32)
    for d in range(8):
        moved = tile if d == 0 else pltpu.roll(tile, PIECE * d, 1)
        diagonal = jnp.sum(jnp.where(lane == sub, moved, 0.0), axis=0, keepdims=True)
        out = jnp.where((lane - sub + 8) % 8 == d, diagonal, out)
    return out


def kernel(
    q_hbm, k_hbm, v_hbm, dk_hbm, dv_hbm, tm_hbm, vl_hbm, out_ref,
    Q, K, V, DK, DV, TM, VL,
    plane, plane_s, xland, xland_s, half_sum, half_s, land, land_s,
    zed, zed_s, zland, zland_s, drafted, drafted_s, final,
    ld, ld_small, q_send, q_recv, c_send, c_recv, n_send, n_recv, a_send, a_recv, z_send, z_recv, g_send, g_recv, o_send, o_recv,
):
    loop_index = lax.axis_index("loop")
    group_index = lax.axis_index("grp")
    core = loop_index % 2
    x = group_index % NX
    z = (group_index // NX) % NZ
    y = (group_index // (NX * NZ)) * 2 + loop_index // 2

    def device(px, py, pz, pc):
        return ((py % 2) * 2 + pc, ((py // 2) * NZ + pz) * NX + px)

    mate = device(x, y, z, 1 - core)

    def in_plane(dx, dy):
        return device((x + dx) % NX, (y + dy) % NY, z, core)

    def piece_of(px, py):
        return px * 2 + py // 2

    mine = piece_of(x, y)

    def remote(src, dst, send, recv, target):
        return pltpu.make_async_remote_copy(
            src_ref=src, dst_ref=dst, send_sem=send, recv_sem=recv, device_id=target, device_id_type=MESH
        )

    lead = z == 0
    peers = [mate, in_plane(0, 1), in_plane(0, 3)]
    peers += [in_plane(dx, dy) for dx, dy in FAR + NEAR if (dx, dy % 2) != (0, 1)]
    others = [device(x, y, other, core) for other in (1, 7, 2, 6, 3, 5, 4)]
    leader = device(x, y, 0, core)
    barrier = pltpu.get_barrier_semaphore()

    def greet(targets):
        for target in targets:
            pl.semaphore_signal(barrier, inc=1, device_id=target, device_id_type=MESH)

    greet(peers)
    pl.when(lead)(lambda: greet(others))
    pl.when(jnp.logical_not(lead))(lambda: greet([leader]))

    def seqs(c):
        return pl.ds(c * PER, PER)

    def load(c):
        return [
            pltpu.make_async_copy(q_hbm.at[seqs(c)], Q.at[0, seqs(c)], ld.at[c, 0]),
            pltpu.make_async_copy(k_hbm.at[seqs(c)], K.at[seqs(c), 0], ld.at[c, 1]),
            pltpu.make_async_copy(v_hbm.at[seqs(c)], V.at[seqs(c), 0], ld.at[c, 2]),
        ]

    small = [
        pltpu.make_async_copy(vl_hbm, VL, ld_small.at[0]),
        pltpu.make_async_copy(dk_hbm, DK, ld_small.at[1]),
        pltpu.make_async_copy(dv_hbm, DV, ld_small.at[2]),
        pltpu.make_async_copy(tm_hbm, TM, ld_small.at[3]),
    ]
    small[0].start()
    for c in range(CHUNKS):
        for copy in load(c):
            copy.start()
    for copy in small[1:]:
        copy.start()

    half = ROWS // 2

    def to_mate(c):
        return [
            remote(k_hbm.at[seqs(c)], K.at[seqs(c), 1], c_send.at[0], c_recv.at[c, 0], mate),
            remote(v_hbm.at[seqs(c)], V.at[seqs(c), 1], c_send.at[1], c_recv.at[c, 1], mate),
        ]

    def ask_far(c, side):
        rows = pl.ds(side * half, half)
        return remote(
            q_hbm.at[seqs(c), rows], Q.at[1, seqs(c), rows], q_send.at[0], q_recv.at[c],
            in_plane(0, 1 if side == 0 else 3),
        )

    def await_far(c):
        remote(Q.at[1, seqs(c)], Q.at[1, seqs(c)], q_send.at[0], q_recv.at[c], mate).wait_recv()

    def first(member):
        return (member * (NX * 2 * NZ) + group_index) * KEYS

    lane = iota((1, 2 * KEYS), 1)
    position = jnp.where(lane < KEYS, first(loop_index), first(loop_index + 1 - 2 * core) - KEYS) + lane
    ones = jnp.ones((2 * KEYS, WIDTH), BF16)
    sub8 = iota((8, ROWS), 0)

    def attend(sides, c):
        def one(i, tiles):
            s = c * PER + i
            values = jnp.concatenate([V[s].reshape(2 * KEYS, WIDTH), ones], axis=1)
            out = []
            for side, tile in zip(sides, tiles):
                scores = lax.dot_general(
                    Q[side, s], K[s].reshape(2 * KEYS, WIDTH), (((1,), (1,)), ((), ())), preferred_element_type=F32
                )
                scores = jnp.where(position < VL[s], scores * SCALE, FLOOR)
                peak = jnp.maximum(jnp.max(scores, axis=1, keepdims=True), LOW)
                weights = jnp.exp2(scores - peak).astype(BF16)
                both = jnp.dot(weights, values, preferred_element_type=F32)
                plane[side, s] = both[:, :WIDTH].astype(BF16)
                tile = jnp.where(sub8 == i, to_row(peak), tile)
                out.append(jnp.where(sub8 == PER + i, to_row(both[:, WIDTH:]), tile))
            return tuple(out)

        tiles = lax.fori_loop(0, PER, one, (jnp.zeros((8, ROWS), F32),) * len(sides), unroll=PER)
        for side, tile in zip(sides, tiles):
            pieces = by_piece(tile)
            for p in range(8):
                plane_s[side, c, p] = pieces[p : p + 1]

    def piece_rows(piece, count=1):
        return pl.ds(pl.multiple_of(piece * PIECE, PIECE), count * PIECE)

    def scatter_x(c):
        copies = []
        for dx in range(1, NX):
            pair = ((x + dx) % NX) * 2
            target = in_plane(dx, 0)
            copies.append(
                remote(plane.at[0, seqs(c), piece_rows(pair, 2)], xland.at[c, dx - 1], n_send.at[0], n_recv.at[c, 0], target)
            )
            copies.append(
                remote(plane_s.at[0, c, pl.ds(pair, 2)], xland_s.at[c, dx - 1], n_send.at[1], n_recv.at[c, 1], target)
            )
        return copies

    def scatter_far(c):
        copies = []
        for n, (dx, dy) in enumerate(FAR):
            piece = piece_of((x + dx) % NX, (y + dy) % NY)
            target = in_plane(dx, dy)
            copies.append(remote(plane.at[1, seqs(c), piece_rows(piece)], land.at[c, n], a_send.at[0], a_recv.at[c, 0], target))
            copies.append(remote(plane_s.at[1, c, piece], land_s.at[c, n], a_send.at[1], a_recv.at[c, 1], target))
        return copies

    def across(c):
        n, target = len(FAR), in_plane(0, 2)
        return [
            remote(half_sum.at[c], land.at[c, n], a_send.at[0], a_recv.at[c, 0], target),
            remote(half_s.at[c], land_s.at[c, n], a_send.at[1], a_recv.at[c, 1], target),
        ]

    def merge(figures, parts):
        peak = jnp.max(figures, axis=0, keepdims=True)
        is_peak = iota((1, ROWS), 1) < SPAN
        factor = jnp.exp2(jnp.where(is_peak, figures - peak, 0.0))
        total = jnp.sum(pltpu.roll(factor, SPAN, 1) * figures, axis=0, keepdims=True)
        acc = jnp.zeros((SPAN, WIDTH), F32)
        for n, part in enumerate(parts):
            acc += part.reshape(SPAN, WIDTH).astype(F32) * to_column(factor[n : n + 1], SPAN, 0)
        return jnp.where(is_peak, peak, total), acc

    def near_sources(c, level):
        piece = x * 2 + level
        rows = pl.ds(pl.multiple_of(level * PIECE, PIECE), PIECE)
        figures = [plane_s[0, c, piece]] + [xland_s[c, n, level] for n in range(NX - 1)]
        parts = [plane[0, seqs(c), piece_rows(piece)]] + [xland[c, n, :, rows] for n in range(NX - 1)]
        return figures, parts

    def merge_across(c):
        remote(xland.at[c], xland.at[c], n_send.at[0], n_recv.at[c, 0], mate).wait_recv()
        remote(xland_s.at[c], xland_s.at[c], n_send.at[1], n_recv.at[c, 1], mate).wait_recv()
        figures, parts = near_sources(c, 1 - y // 2)
        row, acc = merge(jnp.concatenate(figures, axis=0), parts)
        half_s[c] = row
        half_sum[c] = acc.reshape(PER, PIECE, WIDTH).astype(BF16)
        start(across(c))

    def merge_plane(c):
        remote(land.at[c], land.at[c], a_send.at[0], a_recv.at[c, 0], mate).wait_recv()
        remote(land_s.at[c], land_s.at[c], a_send.at[1], a_recv.at[c, 1], mate).wait_recv()
        figures, parts = near_sources(c, y // 2)
        figures += [land_s[c, n] for n in range(len(FAR) + 1)]
        parts += [land[c, n] for n in range(len(FAR) + 1)]
        row, acc = merge(jnp.concatenate(figures, axis=0), parts)
        zed_s[c] = row
        zed[c] = acc.reshape(PER, PIECE, WIDTH).astype(BF16)

    def to_leader(c):
        return [
            remote(zed.at[c], zland.at[c, z - 1], z_send.at[0], z_recv.at[c, 0], leader),
            remote(zed_s.at[c], zland_s.at[c, z - 1], z_send.at[1], z_recv.at[c, 1], leader),
        ]

    def draft(c):
        allowed_rows = pl.ds(pl.multiple_of((mine % 2) * PIECE, PIECE), PIECE)
        for i in range(PER):
            s = c * PER + i
            queries = Q[0, s, piece_rows(mine)]
            scores = lax.dot_general(queries, DK[s], (((1,), (1,)), ((), ())), preferred_element_type=F32) * SCALE
            allowed = TM[s, allowed_rows] == 1
            peak = jnp.max(jnp.where(allowed, scores, FLOOR), axis=1, keepdims=True)
            weights = jnp.where(allowed, jnp.exp2(scores - peak), 0.0).astype(BF16)
            total = jnp.sum(weights.astype(F32), axis=1, keepdims=True)
            rows = pl.ds(i * PIECE, PIECE)
            drafted[c, rows] = jnp.dot(weights, DV[s], preferred_element_type=F32)
            drafted_s[c, 0, rows] = jnp.broadcast_to(peak, (PIECE, WIDTH))
            drafted_s[c, 1, rows] = jnp.broadcast_to(total, (PIECE, WIDTH))

    def finish(c):
        remote(zland.at[c], zland.at[c], z_send.at[0], z_recv.at[c, 0], mate).wait_recv()
        remote(zland_s.at[c], zland_s.at[c], z_send.at[1], z_recv.at[c, 1], mate).wait_recv()
        figures = jnp.concatenate([zed_s[c]] + [zland_s[c, n] for n in range(NZ - 1)], axis=0)
        row, acc = merge(figures, [zed[c]] + [zland[c, n] for n in range(NZ - 1)])
        top, total = to_column(row, SPAN, 0), to_column(row, SPAN, SPAN)
        joined = jnp.maximum(top, drafted_s[c, 0])
        fa, fb = jnp.exp2(top - joined), jnp.exp2(drafted_s[c, 0] - joined)
        result = (acc * fa + drafted[c] * fb) / (total * fa + drafted_s[c, 1] * fb)
        final[c] = result.reshape(PER, PIECE, WIDTH).astype(BF16)

    def from_leader(c, targets):
        return [remote(final.at[c], final.at[c], g_send.at[0], g_recv.at[c], target) for target in targets]

    def keep(c):
        return pltpu.make_async_copy(final.at[c], out_ref.at[seqs(c), piece_rows(mine)], ld.at[c, 0])

    def deliver(c):
        place = out_ref.at[seqs(c), piece_rows(mine)]
        return [remote(final.at[c], place, o_send.at[0], o_recv.at[c], in_plane(dx, dy)) for dx, dy in NEAR]

    def delivered(c):
        part = out_ref.at[seqs(c), pl.ds(0, PIECE * len(NEAR))]
        remote(part, part, o_send.at[0], o_recv.at[c], mate).wait_recv()

    def all_sent(ref, sem):
        remote(ref, ref, sem, sem, mate).wait_send()

    def start(copies):
        for copy in copies:
            copy.start()

    pl.semaphore_wait(barrier, len(peers) + jnp.where(lead, NZ - 1, 1))
    for c in range(CHUNKS):
        for side in range(2):
            ask_far(c, side).start()
    for c in range(CHUNKS):
        start(to_mate(c))

    small[0].wait()

    def near(c):
        for copy in load(c):
            copy.wait()
        for copy in to_mate(c):
            copy.wait_recv()
        attend((0,), c)
        start(scatter_x(c))

    def far(c):
        await_far(c)
        attend((1,), c)
        start(scatter_far(c))

    for c in range(CHUNKS):
        near(c)
    for c in range(CHUNKS):
        far(c)
        merge_across(c)

    all_sent(Q.at[0], q_send.at[0])
    all_sent(K.at[:, 0], c_send.at[0])
    all_sent(V.at[:, 0], c_send.at[1])
    for copy in small[1:]:
        copy.wait()

    @pl.when(lead)
    def _():
        for c in range(CHUNKS):
            draft(c)

    for c in range(CHUNKS):
        merge_plane(c)

        @pl.when(jnp.logical_not(lead))
        def _():
            start(to_leader(c))

    all_sent(xland, n_send.at[0])
    all_sent(xland_s, n_send.at[1])
    all_sent(land, a_send.at[0])
    all_sent(land_s, a_send.at[1])

    for c in range(CHUNKS):

        @pl.when(lead)
        def _():
            finish(c)
            start(from_leader(c, others))

        @pl.when(jnp.logical_not(lead))
        def _():
            from_leader(c, [leader])[0].wait_recv()

        start(deliver(c) + [keep(c)])

    @pl.when(lead)
    def _():
        all_sent(zland, g_send.at[0])

    @pl.when(jnp.logical_not(lead))
    def _():
        all_sent(zed, z_send.at[0])
        all_sent(zed_s, z_send.at[1])

    for c in range(CHUNKS):
        delivered(c)
        keep(c).wait()
    all_sent(zland, o_send.at[0])


def local(queries, cache_keys, cache_values, draft_keys, draft_values, tree_mask, valid_length):
    dma = pltpu.SemaphoreType.DMA
    n = len(FAR) + 1
    scratch = [
        pltpu.VMEM((2, SEQS, ROWS, WIDTH), BF16),
        pltpu.VMEM((SEQS, 2, KEYS, WIDTH), BF16),
        pltpu.VMEM((SEQS, 2, KEYS, WIDTH), BF16),
        pltpu.VMEM((SEQS, DRAFT, WIDTH), BF16),
        pltpu.VMEM((SEQS, DRAFT, WIDTH), BF16),
        pltpu.VMEM((SEQS, DRAFT, DRAFT), jnp.int32),
        pltpu.SMEM((SEQS,), jnp.int32),
        pltpu.VMEM((2, SEQS, ROWS, WIDTH), BF16),
        pltpu.VMEM((2, CHUNKS, 8, 1, ROWS), F32),
        pltpu.VMEM((CHUNKS, NX - 1, PER, 2 * PIECE, WIDTH), BF16),
        pltpu.VMEM((CHUNKS, NX - 1, 2, 1, ROWS), F32),
        pltpu.VMEM((CHUNKS, PER, PIECE, WIDTH), BF16),
        pltpu.VMEM((CHUNKS, 1, ROWS), F32),
        pltpu.VMEM((CHUNKS, n, PER, PIECE, WIDTH), BF16),
        pltpu.VMEM((CHUNKS, n, 1, ROWS), F32),
        pltpu.VMEM((CHUNKS, PER, PIECE, WIDTH), BF16),
        pltpu.VMEM((CHUNKS, 1, ROWS), F32),
        pltpu.VMEM((CHUNKS, NZ - 1, PER, PIECE, WIDTH), BF16),
        pltpu.VMEM((CHUNKS, NZ - 1, 1, ROWS), F32),
        pltpu.VMEM((CHUNKS, SPAN, WIDTH), F32),
        pltpu.VMEM((CHUNKS, 2, SPAN, WIDTH), F32),
        pltpu.VMEM((CHUNKS, PER, PIECE, WIDTH), BF16),
        dma((CHUNKS, 3)),
        dma((4,)),
        dma((1,)),
        dma((CHUNKS,)),
        dma((2,)),
        dma((CHUNKS, 2)),
        dma((2,)),
        dma((CHUNKS, 2)),
        dma((2,)),
        dma((CHUNKS, 2)),
        dma((2,)),
        dma((CHUNKS, 2)),
        dma((1,)),
        dma((CHUNKS,)),
        dma((1,)),
        dma((CHUNKS,)),
    ]
    operands = [
        queries.reshape(SEQS, ROWS, WIDTH),
        cache_keys.reshape(SEQS, KEYS, WIDTH),
        cache_values.reshape(SEQS, KEYS, WIDTH),
        draft_keys.reshape(SEQS, DRAFT, WIDTH),
        draft_values.reshape(SEQS, DRAFT, WIDTH),
        tree_mask,
        valid_length,
    ]
    operands = [pltpu.with_memory_space_constraint(a, pltpu.HBM) for a in operands]
    out = pl.pallas_call(
        kernel,
        out_shape=pltpu.VMEM((SEQS, ROWS, WIDTH), BF16),
        in_specs=[pl.BlockSpec(memory_space=pltpu.HBM)] * 7,
        out_specs=pl.BlockSpec(memory_space=pltpu.VMEM),
        scratch_shapes=scratch,
        compiler_params=pltpu.CompilerParams(collective_id=0, has_side_effects=True, vmem_limit_bytes=40 << 20),
        name="attend",
    )(
        *operands,
    )
    return out.reshape(queries.shape)


def solution(mesh):
    in_specs = (
        P(None, None, "loop", None, None),
        P(None, None, ("loop", "grp"), None),
        P(None, None, ("loop", "grp"), None),
        P(),
        P(),
        P(),
        P(),
    )
    out_specs = P(None, None, "loop", None, None)
    return jax.shard_map(local, mesh=mesh, in_specs=in_specs, out_specs=out_specs, check_vma=False)
```

```python
import math

import jax
import jax.numpy as jnp
from jax import lax
from jax.experimental import pallas as pl
from jax.experimental.pallas import tpu as pltpu
from jax.sharding import PartitionSpec as P

MESH = pl.DeviceIdType.MESH
F32 = jnp.float32
BF16 = jnp.bfloat16

SEQS = 12
ROWS = 128
KEYS = 512
WIDTH = 128
DRAFT = 32
NX, NY, NZ = 4, 4, 8
CHUNKS = 3
PER = SEQS // CHUNKS
PIECE = 16
SPAN = PER * PIECE
NEAR = [(dx, dy) for dy in (2, 0) for dx in (2, 1, 3, 0) if (dx, dy) != (0, 0)]
FAR = [(dx, dy) for dx in (2, 1, 3, 0) for dy in (1, 3)]

SCALE = math.log2(math.e) / math.sqrt(WIDTH)
FLOOR = -1e30
LOW = -1e29


def iota(shape, axis):
    return lax.broadcasted_iota(jnp.int32, shape, axis)


def to_row(column):
    eye = iota((ROWS, ROWS), 0) == iota((ROWS, ROWS), 1)
    return jnp.sum(jnp.where(eye, column, 0.0), axis=0, keepdims=True)


def to_column(row, rows, first):
    pick = iota((rows, ROWS), 1) == iota((rows, ROWS), 0) + first
    return jnp.sum(jnp.where(pick, row, 0.0), axis=1, keepdims=True)


def by_piece(tile):
    lane = iota((8, ROWS), 1) // PIECE
    sub = iota((8, ROWS), 0)
    out = jnp.zeros((8, ROWS), F32)
    for d in range(8):
        moved = tile if d == 0 else pltpu.roll(tile, PIECE * d, 1)
        diagonal = jnp.sum(jnp.where(lane == sub, moved, 0.0), axis=0, keepdims=True)
        out = jnp.where((lane - sub + 8) % 8 == d, diagonal, out)
    return out


def kernel(
    q_hbm, k_hbm, v_hbm, dk_hbm, dv_hbm, tm_hbm, vl_hbm, out_ref,
    Q, K, V, DK, DV, TM, VL,
    plane, plane_s, xland, xland_s, half_sum, half_s, land, land_s,
    zed, zed_s, zland, zland_s, drafted, drafted_s, final,
    ld, ld_small, q_send, q_recv, c_send, c_recv, n_send, n_recv, a_send, a_recv, z_send, z_recv, g_send, g_recv, o_send, o_recv,
):
    loop_index = lax.axis_index("loop")
    group_index = lax.axis_index("grp")
    core = loop_index % 2
    x = group_index % NX
    z = (group_index // NX) % NZ
    y = (group_index // (NX * NZ)) * 2 + loop_index // 2

    def device(px, py, pz, pc):
        return ((py % 2) * 2 + pc, ((py // 2) * NZ + pz) * NX + px)

    mate = device(x, y, z, 1 - core)

    def in_plane(dx, dy):
        return device((x + dx) % NX, (y + dy) % NY, z, core)

    def piece_of(px, py):
        return px * 2 + py // 2

    mine = piece_of(x, y)

    def remote(src, dst, send, recv, target):
        return pltpu.make_async_remote_copy(
            src_ref=src, dst_ref=dst, send_sem=send, recv_sem=recv, device_id=target, device_id_type=MESH
        )

    lead = z == 0
    peers = [mate, in_plane(0, 1), in_plane(0, 3)]
    peers += [in_plane(dx, dy) for dx, dy in FAR + NEAR if (dx, dy % 2) != (0, 1)]
    others = [device(x, y, other, core) for other in (1, 2, 3, 4, 7, 6, 5)]
    leader = device(x, y, 0, core)
    barrier = pltpu.get_barrier_semaphore()

    def greet(targets):
        for target in targets:
            pl.semaphore_signal(barrier, inc=1, device_id=target, device_id_type=MESH)

    greet(peers)
    pl.when(lead)(lambda: greet(others))
    pl.when(jnp.logical_not(lead))(lambda: greet([leader]))

    def seqs(c):
        return pl.ds(c * PER, PER)

    def load(c):
        return [
            pltpu.make_async_copy(q_hbm.at[seqs(c)], Q.at[0, seqs(c)], ld.at[c, 0]),
            pltpu.make_async_copy(k_hbm.at[seqs(c)], K.at[seqs(c), 0], ld.at[c, 1]),
            pltpu.make_async_copy(v_hbm.at[seqs(c)], V.at[seqs(c), 0], ld.at[c, 2]),
        ]

    small = [
        pltpu.make_async_copy(vl_hbm, VL, ld_small.at[0]),
        pltpu.make_async_copy(dk_hbm, DK, ld_small.at[1]),
        pltpu.make_async_copy(dv_hbm, DV, ld_small.at[2]),
        pltpu.make_async_copy(tm_hbm, TM, ld_small.at[3]),
    ]
    small[0].start()
    for c in range(CHUNKS):
        for copy in load(c):
            copy.start()
    for copy in small[1:]:
        copy.start()

    half = ROWS // 2

    def to_mate(c):
        return [
            remote(k_hbm.at[seqs(c)], K.at[seqs(c), 1], c_send.at[0], c_recv.at[c, 0], mate),
            remote(v_hbm.at[seqs(c)], V.at[seqs(c), 1], c_send.at[1], c_recv.at[c, 1], mate),
        ]

    def ask_far(c, side):
        rows = pl.ds(side * half, half)
        return remote(
            q_hbm.at[seqs(c), rows], Q.at[1, seqs(c), rows], q_send.at[0], q_recv.at[c],
            in_plane(0, 1 if side == 0 else 3),
        )

    def await_far(c):
        remote(Q.at[1, seqs(c)], Q.at[1, seqs(c)], q_send.at[0], q_recv.at[c], mate).wait_recv()

    def first(member):
        return (member * (NX * 2 * NZ) + group_index) * KEYS

    lane = iota((1, 2 * KEYS), 1)
    position = jnp.where(lane < KEYS, first(loop_index), first(loop_index + 1 - 2 * core) - KEYS) + lane
    ones = jnp.ones((2 * KEYS, WIDTH), BF16)
    sub8 = iota((8, ROWS), 0)

    def attend(sides, c):
        def one(i, tiles):
            s = c * PER + i
            values = jnp.concatenate([V[s].reshape(2 * KEYS, WIDTH), ones], axis=1)
            out = []
            for side, tile in zip(sides, tiles):
                scores = lax.dot_general(
                    Q[side, s], K[s].reshape(2 * KEYS, WIDTH), (((1,), (1,)), ((), ())), preferred_element_type=F32
                )
                scores = jnp.where(position < VL[s], scores * SCALE, FLOOR)
                peak = jnp.maximum(jnp.max(scores, axis=1, keepdims=True), LOW)
                weights = jnp.exp2(scores - peak).astype(BF16)
                both = jnp.dot(weights, values, preferred_element_type=F32)
                plane[side, s] = both[:, :WIDTH].astype(BF16)
                tile = jnp.where(sub8 == i, to_row(peak), tile)
                out.append(jnp.where(sub8 == PER + i, to_row(both[:, WIDTH:]), tile))
            return tuple(out)

        tiles = lax.fori_loop(0, PER, one, (jnp.zeros((8, ROWS), F32),) * len(sides), unroll=PER)
        for side, tile in zip(sides, tiles):
            pieces = by_piece(tile)
            for p in range(8):
                plane_s[side, c, p] = pieces[p : p + 1]

    def piece_rows(piece, count=1):
        return pl.ds(pl.multiple_of(piece * PIECE, PIECE), count * PIECE)

    def scatter_x(c):
        copies = []
        for dx in (2, 1, 3):
            pair = ((x + dx) % NX) * 2
            target = in_plane(dx, 0)
            copies.append(
                remote(plane.at[0, seqs(c), piece_rows(pair, 2)], xland.at[c, dx - 1], n_send.at[0], n_recv.at[c, 0], target)
            )
            copies.append(
                remote(plane_s.at[0, c, pl.ds(pair, 2)], xland_s.at[c, dx - 1], n_send.at[1], n_recv.at[c, 1], target)
            )
        return copies

    def scatter_far(c):
        copies = []
        for n, (dx, dy) in enumerate(FAR):
            piece = piece_of((x + dx) % NX, (y + dy) % NY)
            target = in_plane(dx, dy)
            copies.append(remote(plane.at[1, seqs(c), piece_rows(piece)], land.at[c, n], a_send.at[0], a_recv.at[c, 0], target))
            copies.append(remote(plane_s.at[1, c, piece], land_s.at[c, n], a_send.at[1], a_recv.at[c, 1], target))
        return copies

    def across(c):
        n, target = len(FAR), in_plane(0, 2)
        return [
            remote(half_sum.at[c], land.at[c, n], a_send.at[0], a_recv.at[c, 0], target),
            remote(half_s.at[c], land_s.at[c, n], a_send.at[1], a_recv.at[c, 1], target),
        ]

    def merge(figures, parts):
        peak = jnp.max(figures, axis=0, keepdims=True)
        is_peak = iota((1, ROWS), 1) < SPAN
        factor = jnp.exp2(jnp.where(is_peak, figures - peak, 0.0))
        total = jnp.sum(pltpu.roll(factor, SPAN, 1) * figures, axis=0, keepdims=True)
        acc = jnp.zeros((SPAN, WIDTH), F32)
        for n, part in enumerate(parts):
            acc += part.reshape(SPAN, WIDTH).astype(F32) * to_column(factor[n : n + 1], SPAN, 0)
        return jnp.where(is_peak, peak, total), acc

    def near_sources(c, level):
        piece = x * 2 + level
        rows = pl.ds(pl.multiple_of(level * PIECE, PIECE), PIECE)
        figures = [plane_s[0, c, piece]] + [xland_s[c, n, level] for n in range(NX - 1)]
        parts = [plane[0, seqs(c), piece_rows(piece)]] + [xland[c, n, :, rows] for n in range(NX - 1)]
        return figures, parts

    def merge_across(c):
        remote(xland.at[c], xland.at[c], n_send.at[0], n_recv.at[c, 0], mate).wait_recv()
        remote(xland_s.at[c], xland_s.at[c], n_send.at[1], n_recv.at[c, 1], mate).wait_recv()
        figures, parts = near_sources(c, 1 - y // 2)
        row, acc = merge(jnp.concatenate(figures, axis=0), parts)
        half_s[c] = row
        half_sum[c] = acc.reshape(PER, PIECE, WIDTH).astype(BF16)
        start(across(c))

    def merge_plane(c):
        remote(land.at[c], land.at[c], a_send.at[0], a_recv.at[c, 0], mate).wait_recv()
        remote(land_s.at[c], land_s.at[c], a_send.at[1], a_recv.at[c, 1], mate).wait_recv()
        figures, parts = near_sources(c, y // 2)
        figures += [land_s[c, n] for n in range(len(FAR) + 1)]
        parts += [land[c, n] for n in range(len(FAR) + 1)]
        row, acc = merge(jnp.concatenate(figures, axis=0), parts)
        zed_s[c] = row
        zed[c] = acc.reshape(PER, PIECE, WIDTH).astype(BF16)

    def to_leader(c):
        return [
            remote(zed.at[c], zland.at[c, z - 1], z_send.at[0], z_recv.at[c, 0], leader),
            remote(zed_s.at[c], zland_s.at[c, z - 1], z_send.at[1], z_recv.at[c, 1], leader),
        ]

    def draft(c):
        allowed_rows = pl.ds(pl.multiple_of((mine % 2) * PIECE, PIECE), PIECE)
        for i in range(PER):
            s = c * PER + i
            queries = Q[0, s, piece_rows(mine)]
            scores = lax.dot_general(queries, DK[s], (((1,), (1,)), ((), ())), preferred_element_type=F32) * SCALE
            allowed = TM[s, allowed_rows] == 1
            peak = jnp.max(jnp.where(allowed, scores, FLOOR), axis=1, keepdims=True)
            weights = jnp.where(allowed, jnp.exp2(scores - peak), 0.0).astype(BF16)
            total = jnp.sum(weights.astype(F32), axis=1, keepdims=True)
            rows = pl.ds(i * PIECE, PIECE)
            drafted[c, rows] = jnp.dot(weights, DV[s], preferred_element_type=F32)
            drafted_s[c, 0, rows] = jnp.broadcast_to(peak, (PIECE, WIDTH))
            drafted_s[c, 1, rows] = jnp.broadcast_to(total, (PIECE, WIDTH))

    def finish(c):
        remote(zland.at[c], zland.at[c], z_send.at[0], z_recv.at[c, 0], mate).wait_recv()
        remote(zland_s.at[c], zland_s.at[c], z_send.at[1], z_recv.at[c, 1], mate).wait_recv()
        figures = jnp.concatenate([zed_s[c]] + [zland_s[c, n] for n in range(NZ - 1)], axis=0)
        row, acc = merge(figures, [zed[c]] + [zland[c, n] for n in range(NZ - 1)])
        top, total = to_column(row, SPAN, 0), to_column(row, SPAN, SPAN)
        joined = jnp.maximum(top, drafted_s[c, 0])
        fa, fb = jnp.exp2(top - joined), jnp.exp2(drafted_s[c, 0] - joined)
        result = (acc * fa + drafted[c] * fb) / (total * fa + drafted_s[c, 1] * fb)
        final[c] = result.reshape(PER, PIECE, WIDTH).astype(BF16)

    def from_leader(c, targets):
        return [remote(final.at[c], final.at[c], g_send.at[0], g_recv.at[c], target) for target in targets]

    def keep(c):
        return pltpu.make_async_copy(final.at[c], out_ref.at[seqs(c), piece_rows(mine)], ld.at[c, 0])

    def deliver(c):
        place = out_ref.at[seqs(c), piece_rows(mine)]
        return [remote(final.at[c], place, o_send.at[0], o_recv.at[c], in_plane(dx, dy)) for dx, dy in NEAR]

    def delivered(c):
        part = out_ref.at[seqs(c), pl.ds(0, PIECE * len(NEAR))]
        remote(part, part, o_send.at[0], o_recv.at[c], mate).wait_recv()

    def all_sent(ref, sem):
        remote(ref, ref, sem, sem, mate).wait_send()

    def start(copies):
        for copy in copies:
            copy.start()

    pl.semaphore_wait(barrier, len(peers) + jnp.where(lead, NZ - 1, 1))
    for c in range(CHUNKS):
        for side in range(2):
            ask_far(c, side).start()
    for c in range(CHUNKS):
        start(to_mate(c))

    small[0].wait()

    def near(c):
        for copy in load(c):
            copy.wait()
        for copy in to_mate(c):
            copy.wait_recv()
        attend((0,), c)
        start(scatter_x(c))

    def far(c):
        await_far(c)
        attend((1,), c)
        start(scatter_far(c))

    for c in range(CHUNKS):
        near(c)
    for c in range(CHUNKS):
        far(c)
        merge_across(c)

    all_sent(Q.at[0], q_send.at[0])
    all_sent(K.at[:, 0], c_send.at[0])
    all_sent(V.at[:, 0], c_send.at[1])
    for copy in small[1:]:
        copy.wait()

    @pl.when(lead)
    def _():
        for c in range(CHUNKS):
            draft(c)

    for c in range(CHUNKS):
        merge_plane(c)

        @pl.when(jnp.logical_not(lead))
        def _():
            start(to_leader(c))

    all_sent(xland, n_send.at[0])
    all_sent(xland_s, n_send.at[1])
    all_sent(land, a_send.at[0])
    all_sent(land_s, a_send.at[1])

    for c in range(CHUNKS):

        @pl.when(lead)
        def _():
            finish(c)
            start(from_leader(c, others))

        @pl.when(jnp.logical_not(lead))
        def _():
            from_leader(c, [leader])[0].wait_recv()

        start(deliver(c) + [keep(c)])

    @pl.when(lead)
    def _():
        all_sent(zland, g_send.at[0])

    @pl.when(jnp.logical_not(lead))
    def _():
        all_sent(zed, z_send.at[0])
        all_sent(zed_s, z_send.at[1])

    for c in range(CHUNKS):
        delivered(c)
        keep(c).wait()
    all_sent(zland, o_send.at[0])


def local(queries, cache_keys, cache_values, draft_keys, draft_values, tree_mask, valid_length):
    dma = pltpu.SemaphoreType.DMA
    n = len(FAR) + 1
    scratch = [
        pltpu.VMEM((2, SEQS, ROWS, WIDTH), BF16),
        pltpu.VMEM((SEQS, 2, KEYS, WIDTH), BF16),
        pltpu.VMEM((SEQS, 2, KEYS, WIDTH), BF16),
        pltpu.VMEM((SEQS, DRAFT, WIDTH), BF16),
        pltpu.VMEM((SEQS, DRAFT, WIDTH), BF16),
        pltpu.VMEM((SEQS, DRAFT, DRAFT), jnp.int32),
        pltpu.SMEM((SEQS,), jnp.int32),
        pltpu.VMEM((2, SEQS, ROWS, WIDTH), BF16),
        pltpu.VMEM((2, CHUNKS, 8, 1, ROWS), F32),
        pltpu.VMEM((CHUNKS, NX - 1, PER, 2 * PIECE, WIDTH), BF16),
        pltpu.VMEM((CHUNKS, NX - 1, 2, 1, ROWS), F32),
        pltpu.VMEM((CHUNKS, PER, PIECE, WIDTH), BF16),
        pltpu.VMEM((CHUNKS, 1, ROWS), F32),
        pltpu.VMEM((CHUNKS, n, PER, PIECE, WIDTH), BF16),
        pltpu.VMEM((CHUNKS, n, 1, ROWS), F32),
        pltpu.VMEM((CHUNKS, PER, PIECE, WIDTH), BF16),
        pltpu.VMEM((CHUNKS, 1, ROWS), F32),
        pltpu.VMEM((CHUNKS, NZ - 1, PER, PIECE, WIDTH), BF16),
        pltpu.VMEM((CHUNKS, NZ - 1, 1, ROWS), F32),
        pltpu.VMEM((CHUNKS, SPAN, WIDTH), F32),
        pltpu.VMEM((CHUNKS, 2, SPAN, WIDTH), F32),
        pltpu.VMEM((CHUNKS, PER, PIECE, WIDTH), BF16),
        dma((CHUNKS, 3)),
        dma((4,)),
        dma((1,)),
        dma((CHUNKS,)),
        dma((2,)),
        dma((CHUNKS, 2)),
        dma((2,)),
        dma((CHUNKS, 2)),
        dma((2,)),
        dma((CHUNKS, 2)),
        dma((2,)),
        dma((CHUNKS, 2)),
        dma((1,)),
        dma((CHUNKS,)),
        dma((1,)),
        dma((CHUNKS,)),
    ]
    operands = [
        queries.reshape(SEQS, ROWS, WIDTH),
        cache_keys.reshape(SEQS, KEYS, WIDTH),
        cache_values.reshape(SEQS, KEYS, WIDTH),
        draft_keys.reshape(SEQS, DRAFT, WIDTH),
        draft_values.reshape(SEQS, DRAFT, WIDTH),
        tree_mask,
        valid_length,
    ]
    operands = [pltpu.with_memory_space_constraint(a, pltpu.HBM) for a in operands]
    out = pl.pallas_call(
        kernel,
        out_shape=pltpu.VMEM((SEQS, ROWS, WIDTH), BF16),
        in_specs=[pl.BlockSpec(memory_space=pltpu.HBM)] * 7,
        out_specs=pl.BlockSpec(memory_space=pltpu.VMEM),
        scratch_shapes=scratch,
        compiler_params=pltpu.CompilerParams(collective_id=0, has_side_effects=True, vmem_limit_bytes=40 << 20),
        name="attend",
    )(
        *operands,
    )
    return out.reshape(queries.shape)


def solution(mesh):
    in_specs = (
        P(None, None, "loop", None, None),
        P(None, None, ("loop", "grp"), None),
        P(None, None, ("loop", "grp"), None),
        P(),
        P(),
        P(),
        P(),
    )
    out_specs = P(None, None, "loop", None, None)
    return jax.shard_map(local, mesh=mesh, in_specs=in_specs, out_specs=out_specs, check_vma=False)
```
